256 devices in a mesh: energy: 64 (over z, y_lo, x), cuts: 4 (over y_hi, core).
Axes of the slice: x: 4, y: 4 (y_hi: 2, y_lo: 2; y = y_hi * 2 + y_lo), z: 8, core: 2. Of those that a mesh axis runs over, the one named last changes fastest.
Arguments:
- lesser: bfloat16 [128, 4, 2, 512, 512], P('energy', 'cuts'), may hold values from -6 to 6
- greater: bfloat16 [128, 4, 2, 512, 512], P('energy', 'cuts'), may hold values from -6 to 6
- couplings: bfloat16 [4, 3, 512, 512], P('cuts'), may hold values from -0.25 to 0.25
- rim_couple: bfloat16 [4, 2, 128, 128], P('cuts'), may hold values from -0.5 to 0.5
- bose_factor: float32 [3], replicated, may hold values from 0.05 to 2
- offsets: int32 [3], replicated, may hold values from 1 to 2, as said below
- pattern: int32 [4, 3], replicated, may hold values from 0 to 1, as said below
Outputs:
- sigma_lesser: bfloat16 [128, 4, 2, 512, 512], P('energy', 'cuts')
- sigma_retarded: bfloat16 [128, 4, 2, 512, 512], P('energy', 'cuts')
The draws below stay inside these ranges and needn't reach their ends.
Inputs may be any that keep to these rules, and one draw needn't show every extreme that they name: `offsets`: one mode's shift is exactly 2. `pattern`: each block couples to 1 to 3 modes. In every draw one block couples to all 3 modes and the other block of its aligned pair (blocks 2i and 2i + 1) to exactly one.
All inputs are finite; a program needn't handle non-finite values.
Results may differ from the reference program's by a relative error of at most 0.0057.
Values may be sent and summed in bfloat16 or wider, within the bound.
No kernel may reach another device: no remote copies, remote signals or barrier semaphores. Data moves between devices by JAX's collectives and lax.ppermute only.
A program may use at most 128 MiB of HBM per device.

```python
import math
import jax
import jax.numpy as jnp
from jax import lax

N = 512
RIM = 128
MODES = 3
E_DEV = 2
ENERGIES = 128
BLOCKS = 4


def draw_offsets(key, part):
    key = jax.random.fold_in(key, 11)
    first_key, second_key = jax.random.split(key)
    values = jax.random.randint(first_key, (MODES,), 1, E_DEV + 1)
    chosen = jax.random.randint(second_key, (), 0, MODES)
    return jnp.where(jnp.arange(MODES) == chosen, E_DEV, values).astype(jnp.int32)


def draw_pattern(key, part):
    key = jax.random.fold_in(key, 23)
    bits_key, keep_key, full_key, single_key = jax.random.split(key, 4)
    bits = jax.random.randint(bits_key, (BLOCKS, MODES), 0, 2)
    keeper = jax.random.randint(keep_key, (BLOCKS,), 0, MODES)
    column = jnp.arange(MODES)[None, :]
    bits = jnp.where(column == keeper[:, None], 1, bits)
    full_block = jax.random.randint(full_key, (), 0, BLOCKS)
    lone_block = full_block + 1 - 2 * (full_block % 2)
    single_mode = jax.random.randint(single_key, (), 0, MODES)
    block_rows = jnp.arange(BLOCKS)[:, None]
    bits = jnp.where(block_rows == full_block, 1, bits)
    bits = jnp.where(block_rows == lone_block, (column == single_mode).astype(jnp.int32), bits)
    return bits.astype(jnp.int32)


def level_of(stream_key, extent, cuts, least, top_value):
    loudness = 1.0
    for axis_at, shards_of in cuts:
        draws = jax.random.uniform(jax.random.fold_in(jax.random.fold_in(stream_key, 6), axis_at), (shards_of,), jnp.float32, least / len(cuts), top_value / len(cuts))
        loudness = loudness * jnp.repeat(jnp.exp(draws), extent[axis_at] // shards_of).reshape((-1,) + (1,) * (len(extent) - 1 - axis_at))
    return loudness


def bell_draw(rng, shape, deviation, limit, pieces=(), held_as=jnp.bfloat16):
    result = jax.random.normal(rng, shape, jnp.float32) * deviation
    if len(pieces) > 0:
        result = level_of(rng, shape, pieces, -0.22, 0.18) * result
    return jnp.clip(result, min=-limit, max=limit).astype(held_as)


def setup_inputs(seed: int = 0) -> dict:
    seeds = jax.random.split(jax.random.key(seed), 8)
    return {
        "lesser": bell_draw(seeds[0], (ENERGIES, BLOCKS, 2, N, N), 1.0, 6.0, ((0, 64), (1, 4))),
        "greater": bell_draw(seeds[1], (ENERGIES, BLOCKS, 2, N, N), 1.0, 6.0, ((0, 64), (1, 4))),
        "couplings": bell_draw(seeds[2], (BLOCKS, MODES, N, N), N ** -0.5, 0.25, ((0, 4),)),
        "rim_couple": bell_draw(seeds[3], (BLOCKS, 2, RIM, RIM), RIM ** -0.5, 0.5, ((0, 4),)),
        "bose_factor": jnp.clip(jnp.exp(jax.random.uniform(seeds[4], (MODES,), jnp.float32, math.log(0.05), math.log(2.0))), 0.05, 2.0),
        "offsets": draw_offsets(jax.random.fold_in(seeds[7], 71), 0),
        "pattern": draw_pattern(jax.random.fold_in(seeds[7], 71), 0),
    }


def mix_shift(ahead_green, behind, weight):
    lead_weight = jnp.stack([weight + 1.0, weight]).astype(jnp.float32)
    trail_weight = jnp.stack([weight, weight + 1.0]).astype(jnp.float32)
    mixed_green = lead_weight[None, :, None, None, None] * ahead_green.astype(jnp.float32) + trail_weight[None, :, None, None, None] * behind.astype(jnp.float32)
    return mixed_green.astype(jnp.bfloat16)


def sandwich(matrix, mixed_green):
    left_product = jnp.einsum('ij,etpjk->etpik', matrix.astype(jnp.float32), mixed_green.astype(jnp.float32), precision=lax.Precision.HIGHEST).astype(jnp.bfloat16)
    return jnp.einsum('etpij,kj->etpik', left_product.astype(jnp.float32), matrix.astype(jnp.float32), precision=lax.Precision.HIGHEST)


def reference(lesser, greater, couplings, rim_couple, bose_factor, offsets, pattern):
    green_pair = jnp.concatenate([lesser[:, :, None], greater[:, :, None]], 2)
    corners = green_pair[:, :, :, :, N - RIM:, N - RIM:]
    from_low = jnp.concatenate([jnp.zeros_like(corners[:, :1]), corners[:, :-1]], 1)
    top_corners = green_pair[:, :, :, :, :RIM, :RIM]
    from_high = jnp.concatenate([top_corners[:, 1:], jnp.zeros_like(top_corners[:, :1])], 1)

    def one_block(block_index):
        block_green = lax.dynamic_index_in_dim(green_pair, block_index, 1, keepdims=False)
        mode_flags = lax.dynamic_index_in_dim(pattern, block_index, 0, keepdims=False)
        mode_couplings = lax.dynamic_index_in_dim(couplings, block_index, 0, keepdims=False)
        couple = lax.dynamic_index_in_dim(rim_couple, block_index, 0, keepdims=False)
        zero_pad = jnp.zeros((E_DEV,) + block_green.shape[1:], block_green.dtype)
        padded = jnp.concatenate([zero_pad, block_green, zero_pad], 0)
        accumulated = jnp.zeros(block_green.shape, jnp.float32)
        for mode_index in range(MODES):
            shift = offsets[mode_index].astype(jnp.int32)
            ahead_green = lax.dynamic_slice_in_dim(padded, (E_DEV + shift).astype(jnp.int32), ENERGIES, 0)
            behind = lax.dynamic_slice_in_dim(padded, (E_DEV - shift).astype(jnp.int32), ENERGIES, 0)
            mixed_green = mix_shift(ahead_green, behind, bose_factor[mode_index])
            accumulated = accumulated + mode_flags[mode_index].astype(jnp.float32) * sandwich(mode_couplings[mode_index], mixed_green)
        low_part = lax.dynamic_index_in_dim(from_low, block_index, 1, keepdims=False)
        high_part = lax.dynamic_index_in_dim(from_high, block_index, 1, keepdims=False)
        accumulated = accumulated.at[:, :, :, :RIM, :RIM].add(sandwich(couple[0], low_part))
        accumulated = accumulated.at[:, :, :, N - RIM:, N - RIM:].add(sandwich(couple[1], high_part))
        lesser_part = accumulated[:, 0]
        retarded = 0.5 * (accumulated[:, 1] - accumulated[:, 0])
        return lesser_part.astype(jnp.bfloat16), retarded.astype(jnp.bfloat16)

    lesser_blocks, retarded_blocks = lax.map(one_block, jnp.arange(BLOCKS, dtype=jnp.int32))
    return jnp.swapaxes(lesser_blocks, 0, 1), jnp.swapaxes(retarded_blocks, 0, 1)
```

```python
import jax
import jax.numpy as jnp
from jax import lax
from jax.experimental import pallas as pl
from jax.experimental.pallas import tpu as pltpu
from jax.sharding import PartitionSpec as P


def shifted(x, energies, cuts, first):
    pairs = []
    for e in range(energies):
        for c in range(cuts):
            up = (c % 2 == 0) == first
            to = e + 1 if up else e - 1
            if 0 <= to < energies:
                pairs.append((e * cuts + c, to * cuts + c))
    return lax.ppermute(x, ("energy", "cuts"), pairs)


def passed_along(x, axis, by):
    length = lax.axis_size(axis)
    pairs = [(i, i + by) for i in range(length) if 0 <= i + by < length]
    return lax.ppermute(x, axis, pairs)


def product(a, b):
    return lax.dot_general(a, b, (((1,), (0,)), ((), ())), preferred_element_type=jnp.float32)


def product_t(a, b):
    return lax.dot_general(a, b, (((1,), (1,)), ((), ())), preferred_element_type=jnp.float32)


def far_kernel(slot, place, offsets, pattern, bose, lesser, greater, couple, low_out, ret_out, total):
    cut, core = place[0], place[1]
    energy = core if slot == 0 else 1 - core
    modes = couple.shape[1]
    total[...] = jnp.zeros_like(total)
    for mode in range(modes):

        @pl.when((pattern[cut, mode] > 0) & (offsets[mode] == 2))
        def _():
            matrix = couple[0, mode]
            for kind, green in enumerate((lesser, greater)):
                weight = bose[mode] + jnp.where(energy == kind, 0.0, 1.0)
                mixed = (green[0, 0, 0].astype(jnp.float32) * weight).astype(jnp.bfloat16)
                left = product(matrix, mixed).astype(jnp.bfloat16)
                total[kind] += product_t(left, matrix)

    low_out[0] = total[0].astype(jnp.bfloat16)
    ret_out[0] = (0.5 * (total[1] - total[0])).astype(jnp.bfloat16)


def far_terms(slot, scalars, bose, lesser, greater, couplings):
    orbitals = lesser.shape[-1]
    parts = lesser.shape[2]
    modes = couplings.shape[1]

    def green_at(p, place, *_):
        return (place[1] if slot == 0 else 1 - place[1], 0, p, 0, 0)

    green = pl.BlockSpec((1, 1, 1, orbitals, orbitals), green_at)
    out = pl.BlockSpec((1, orbitals, orbitals), lambda p, *_: (p, 0, 0))
    kernel = lambda *refs: far_kernel(slot, *refs)
    return pl.pallas_call(
        kernel,
        grid_spec=pltpu.PrefetchScalarGridSpec(
            num_scalar_prefetch=4,
            grid=(parts,),
            in_specs=[
                green,
                green,
                pl.BlockSpec((1, modes, orbitals, orbitals), lambda p, *_: (0, 0, 0, 0)),
            ],
            out_specs=[out, out],
            scratch_shapes=[pltpu.VMEM((2, orbitals, orbitals), jnp.float32)],
        ),
        out_shape=[jax.ShapeDtypeStruct((parts, orbitals, orbitals), jnp.bfloat16)] * 2,
        compiler_params=pltpu.CompilerParams(vmem_limit_bytes=40 * 2**20),
        cost_estimate=pl.CostEstimate(
            flops=parts * 2 * modes * 4 * orbitals**3, bytes_accessed=6 * 2**20, transcendentals=0
        ),
        name="far_terms",
    )(*scalars, bose, lesser, greater, couplings)


def near_kernel(
    place, offsets, pattern, bose,
    lesser, greater, first_low, first_high, second_low, second_high,
    corner_low, corner_high, couple, rim, low_out, ret_out, total,
):
    cut, core = place[0], place[1]
    slot = pl.program_id(1)
    energy = jnp.where(slot == 0, core, 1 - core)
    modes = couple.shape[1]
    orbitals = couple.shape[-1]
    width = rim.shape[-1]
    greens = (lesser, greater)
    first = (first_low, first_high)
    second = (second_low, second_high)
    total[...] = jnp.zeros_like(total)
    for mode in range(modes):
        here = pattern[cut, mode] > 0
        wide = offsets[mode] == 2

        @pl.when(here)
        def _():
            matrix = couple[0, mode]
            for kind in range(2):
                same = bose[mode] + jnp.where(energy == kind, 1.0, 0.0)
                other = bose[mode] + jnp.where(energy == kind, 0.0, 1.0)
                own = jnp.where(wide, 0.0, same)
                cross = jnp.where(wide, same, other)
                use_first = wide == (slot == 1)
                a = jnp.where(use_first, cross, 0.0)
                b = jnp.where(use_first, 0.0, cross)
                mixed = (
                    greens[kind][0, 0, 0].astype(jnp.float32) * own
                    + first[kind][0, 0, 0].astype(jnp.float32) * a
                    + second[kind][0, 0, 0].astype(jnp.float32) * b
                ).astype(jnp.bfloat16)
                left = product(matrix, mixed).astype(jnp.bfloat16)
                total[kind] += product_t(left, matrix)

    for kind in range(2):
        for side, corner in enumerate((corner_low, corner_high)):
            matrix = rim[0, side]
            left = product(matrix, corner[0, kind, 0]).astype(jnp.bfloat16)
            at = slice(0, width) if side == 0 else slice(orbitals - width, orbitals)
            total[kind, at, at] += product_t(left, matrix)
    low_out[0, 0] = total[0]
    ret_out[0, 0] = 0.5 * (total[1] - total[0])


def near_terms(scalars, bose, lesser, greater, near, corners, couplings, rim_couple):
    orbitals = lesser.shape[-1]
    parts = lesser.shape[2]
    modes = couplings.shape[1]
    width = rim_couple.shape[-1]

    def energy_of(j, place):
        return jnp.where(j == 0, place[1], 1 - place[1])

    own = pl.BlockSpec(
        (1, 1, 1, orbitals, orbitals), lambda p, j, place, *_: (1 - energy_of(j, place), 0, p, 0, 0)
    )
    arrived = pl.BlockSpec((1, 1, 1, orbitals, orbitals), lambda p, j, *_: (0, 0, p, 0, 0))
    corner = pl.BlockSpec(
        (1, 2, 1, width, width), lambda p, j, place, *_: (energy_of(j, place), 0, p, 0, 0)
    )
    out = pl.BlockSpec((1, 1, orbitals, orbitals), lambda p, j, *_: (j, p, 0, 0))
    return pl.pallas_call(
        near_kernel,
        grid_spec=pltpu.PrefetchScalarGridSpec(
            num_scalar_prefetch=4,
            grid=(parts, 2),
            in_specs=[own, own, arrived, arrived, arrived, arrived, corner, corner]
            + [
                pl.BlockSpec((1, modes, orbitals, orbitals), lambda p, j, *_: (0, 0, 0, 0)),
                pl.BlockSpec((1, 2, width, width), lambda p, j, *_: (0, 0, 0, 0)),
            ],
            out_specs=[out, out],
            scratch_shapes=[pltpu.VMEM((2, orbitals, orbitals), jnp.float32)],
        ),
        out_shape=[jax.ShapeDtypeStruct((2, parts, orbitals, orbitals), jnp.float32)] * 2,
        compiler_params=pltpu.CompilerParams(vmem_limit_bytes=40 * 2**20),
        cost_estimate=pl.CostEstimate(
            flops=parts * 4 * modes * 4 * orbitals**3, bytes_accessed=20 * 2**20, transcendentals=0
        ),
        name="near_terms",
    )(*scalars, bose, lesser, greater, *near, *corners, couplings, rim_couple)


def add_kernel(place, near, far_first, far_second, out):
    core = place[1]
    out[core, 0, 0] = (near[0, 0] + far_first[0].astype(jnp.float32)).astype(out.dtype)
    out[1 - core, 0, 0] = (near[1, 0] + far_second[0].astype(jnp.float32)).astype(out.dtype)


def added(place, near, far_first, far_second):
    parts, orbitals = near.shape[1], near.shape[-1]
    rows = orbitals // 2
    far = pl.BlockSpec((1, rows, orbitals), lambda p, r, *_: (p, r, 0))
    return pl.pallas_call(
        add_kernel,
        grid_spec=pltpu.PrefetchScalarGridSpec(
            num_scalar_prefetch=1,
            grid=(parts, orbitals // rows),
            in_specs=[
                pl.BlockSpec((2, 1, rows, orbitals), lambda p, r, *_: (0, p, r, 0)),
                far,
                far,
            ],
            out_specs=pl.BlockSpec((2, 1, 1, rows, orbitals), lambda p, r, *_: (0, 0, p, r, 0)),
        ),
        out_shape=jax.ShapeDtypeStruct((2, 1, parts, orbitals, orbitals), jnp.bfloat16),
        compiler_params=pltpu.CompilerParams(vmem_limit_bytes=24 * 2**20),
        cost_estimate=pl.CostEstimate(
            flops=4 * orbitals**2, bytes_accessed=8 * 2**20, transcendentals=0
        ),
        name="added",
    )(place, near, far_first, far_second)


def body(lesser, greater, couplings, rim_couple, bose_factor, offsets, pattern):
    energies = lax.axis_size("energy")
    cuts = lax.axis_size("cuts")
    orbitals = lesser.shape[-1]
    rim_width = rim_couple.shape[-1]
    cut = lax.axis_index("cuts")
    core = cut % 2
    place = jnp.stack([cut, core]).astype(jnp.int32)
    scalars = (place, offsets, pattern)

    near = []
    for first in (True, False):
        for green in (lesser, greater):
            sent = lax.dynamic_slice_in_dim(green, 1 - core if first else core, 1, 0)
            near.append(shifted(sent, energies, cuts, first))

    corners = []
    for by in (1, -1):
        edge = slice(orbitals - rim_width, orbitals) if by == 1 else slice(0, rim_width)
        sent = jnp.concatenate([lesser[..., edge, edge], greater[..., edge, edge]], 1)
        corners.append(passed_along(sent, "cuts", by))

    far_low, far_ret = [], []
    for slot in range(2):
        low, ret = far_terms(slot, scalars, bose_factor, lesser, greater, couplings)
        far_low.append(shifted(low, energies, cuts, slot == 0))
        far_ret.append(shifted(ret, energies, cuts, slot == 0))

    low, ret = near_terms(
        scalars, bose_factor, lesser, greater, near, corners, couplings, rim_couple
    )
    return added(place, low, *far_low), added(place, ret, *far_ret)


def solution(mesh):
    return jax.shard_map(
        body,
        mesh=mesh,
        in_specs=(
            P("energy", "cuts", None, None, None),
            P("energy", "cuts", None, None, None),
            P("cuts", None, None, None),
            P("cuts", None, None, None),
            P(),
            P(),
            P(),
        ),
        out_specs=(P("energy", "cuts", None, None, None), P("energy", "cuts", None, None, None)),
        check_vma=False,
    )
```

```python
import functools

import jax
import jax.numpy as jnp
from jax import lax
from jax.experimental import pallas as pl
from jax.experimental.pallas import tpu as pltpu
from jax.sharding import PartitionSpec as P


def swapped(x, energies, cuts, inside):
    pairs = []
    for e in range(energies):
        for c in range(cuts):
            to = c ^ 1 if inside else (c + 1 if c % 2 else c - 1)
            if 0 <= to < cuts:
                pairs.append((e * cuts + c, e * cuts + to))
    return lax.ppermute(x, ("energy", "cuts"), pairs)


def shifted(x, energies, cuts, first):
    pairs = []
    for e in range(energies):
        for c in range(cuts):
            up = (c % 2 == 0) == first
            to = e + 1 if up else e - 1
            if 0 <= to < energies:
                pairs.append((e * cuts + c, to * cuts + c))
    return lax.ppermute(x, ("energy", "cuts"), pairs)


def product(a, b):
    return lax.dot_general(a, b, (((1,), (0,)), ((), ())), preferred_element_type=jnp.float32)


def product_t(a, b):
    return lax.dot_general(a, b, (((1,), (1,)), ((), ())), preferred_element_type=jnp.float32)


def run_copies(pairs, sems):
    copies = [pltpu.make_async_copy(src, dst, sems.at[i]) for i, (src, dst) in enumerate(pairs)]
    for copy in copies:
        copy.start()
    for copy in copies:
        copy.wait()


def corner_kernel(width, place, lesser, greater, inner, outer, sems):
    core = place[1]
    span = lesser.shape[-1] - width
    pairs = []
    for kind, green in enumerate((lesser, greater)):
        for far_side, out in ((core, outer), (1 - core, inner)):
            edge = pl.ds(pl.multiple_of(far_side * span, width), width)
            pairs.append((green.at[:, 0, :, edge, edge], out.at[:, kind]))
    run_copies(pairs, sems)


def near_copy_kernel(first, place, lesser, greater, near, sems):
    at = 1 - place[1] if first else place[1]
    greens = enumerate((lesser, greater))
    run_copies([(green.at[at, 0], near.at[kind]) for kind, green in greens], sems)


def copied(kernel, shapes, copies, place, lesser, greater):
    anywhere = pl.BlockSpec(memory_space=pl.ANY)
    return pl.pallas_call(
        kernel,
        grid_spec=pltpu.PrefetchScalarGridSpec(
            num_scalar_prefetch=1,
            grid=(),
            in_specs=[anywhere, anywhere],
            out_specs=[anywhere] * len(shapes),
            scratch_shapes=[pltpu.SemaphoreType.DMA((copies,))],
        ),
        out_shape=[jax.ShapeDtypeStruct(shape, lesser.dtype) for shape in shapes],
        compiler_params=pltpu.CompilerParams(vmem_limit_bytes=60 * 2**20),
        cost_estimate=pl.CostEstimate(flops=0, bytes_accessed=4 * 2**20, transcendentals=0),
        name="copied",
    )(place, lesser, greater)


def far_kernel(slot, place, offsets, pattern, bose, lesser, greater, couple, bulk, rest, total):
    cut, core = place[0], place[1]
    part = pl.program_id(0)
    energy = core if slot == 0 else 1 - core
    modes, orbitals = couple.shape[1], couple.shape[2]
    half = rest.shape[0]
    total[...] = jnp.zeros_like(total)
    for mode in range(modes):

        @pl.when((pattern[cut, mode] > 0) & (offsets[mode] == 2))
        def _():
            matrix = couple[0, mode]
            for kind, green in enumerate((lesser, greater)):
                weight = bose[mode] + jnp.where(energy == kind, 0.0, 1.0)
                left = (product(matrix, green[0, 0, 0]) * weight).astype(jnp.bfloat16)
                total[kind] += product_t(left, matrix)

    low = total[0].astype(jnp.bfloat16)
    ret = (0.5 * (total[1] - total[0])).astype(jnp.bfloat16)

    @pl.when(part == 0)
    def _():
        bulk[:orbitals] = low
        bulk[2 * orbitals : 3 * orbitals] = ret

    @pl.when(part == 1)
    def _():
        bulk[orbitals : 2 * orbitals] = low
        bulk[3 * orbitals :] = ret[: orbitals - half]
        rest[...] = ret[orbitals - half :]


def far_terms(slot, scalars, bose, lesser, greater, couplings):
    orbitals = lesser.shape[-1]
    parts = lesser.shape[2]
    modes = couplings.shape[1]
    half = orbitals // 2

    def green_at(p, place, *_):
        return (place[1] if slot == 0 else 1 - place[1], 0, p, 0, 0)

    green = pl.BlockSpec((1, 1, 1, orbitals, orbitals), green_at)
    shapes = [(4 * orbitals - half, orbitals), (half, orbitals)]
    kernel = lambda *refs: far_kernel(slot, *refs)
    return pl.pallas_call(
        kernel,
        grid_spec=pltpu.PrefetchScalarGridSpec(
            num_scalar_prefetch=4,
            grid=(parts,),
            in_specs=[
                green,
                green,
                pl.BlockSpec((1, modes, orbitals, orbitals), lambda p, *_: (0, 0, 0, 0)),
            ],
            out_specs=[pl.BlockSpec(shape, lambda p, *_: (0, 0)) for shape in shapes],
            scratch_shapes=[pltpu.VMEM((2, orbitals, orbitals), jnp.float32)],
        ),
        out_shape=[jax.ShapeDtypeStruct(shape, jnp.bfloat16) for shape in shapes],
        compiler_params=pltpu.CompilerParams(vmem_limit_bytes=32 * 2**20),
        cost_estimate=pl.CostEstimate(
            flops=parts * 2 * modes * 16 * orbitals**3, bytes_accessed=6 * 2**20, transcendentals=0
        ),
        name="far_terms",
    )(*scalars, bose, lesser, greater, couplings)


def near_kernel(
    place, offsets, pattern, bose,
    lesser, greater, first, second, inner, outer, couple, rim, low_out, ret_out, total,
):
    cut, core = place[0], place[1]
    slot = pl.program_id(1)
    energy = jnp.where(slot == 0, core, 1 - core)
    modes = couple.shape[1]
    orbitals = couple.shape[-1]
    width = rim.shape[-1]
    greens = (lesser, greater)
    total[...] = jnp.zeros_like(total)

    def wide_term(mode, arrived):
        matrix = couple[0, mode]
        for kind in range(2):
            weight = bose[mode] + jnp.where(energy == kind, 1.0, 0.0)
            left = (product(matrix, arrived[kind, 0]) * weight).astype(jnp.bfloat16)
            total[kind] += product_t(left, matrix)

    def narrow_term(mode, arrived):
        matrix = couple[0, mode]
        for kind in range(2):
            own = bose[mode] + jnp.where(energy == kind, 1.0, 0.0)
            other = bose[mode] + jnp.where(energy == kind, 0.0, 1.0)
            mixed = (
                greens[kind][0, 0, 0].astype(jnp.float32) * own
                + arrived[kind, 0].astype(jnp.float32) * other
            ).astype(jnp.bfloat16)
            left = product(matrix, mixed).astype(jnp.bfloat16)
            total[kind] += product_t(left, matrix)

    for mode in range(modes):
        here = pattern[cut, mode] > 0
        wide = offsets[mode] == 2
        for at, arrived in enumerate((first, second)):
            pl.when(here & wide & (slot != at))(lambda m=mode, a=arrived: wide_term(m, a))
            pl.when(here & ~wide & (slot == at))(lambda m=mode, a=arrived: narrow_term(m, a))

    for kind in range(2):
        for side in range(2):
            matrix = rim[0, side]
            corner = jnp.where(core == side, outer[0, kind, 0], inner[0, kind, 0])
            left = product(matrix, corner).astype(jnp.bfloat16)
            at = slice(0, width) if side == 0 else slice(orbitals - width, orbitals)
            total[kind, at, at] += product_t(left, matrix)
    low_out[0, 0] = total[0]
    ret_out[0, 0] = 0.5 * (total[1] - total[0])


def near_terms(scalars, bose, lesser, greater, near, corners, couplings, rim_couple):
    orbitals = lesser.shape[-1]
    parts = lesser.shape[2]
    modes = couplings.shape[1]
    width = rim_couple.shape[-1]

    def energy_of(j, place):
        return jnp.where(j == 0, place[1], 1 - place[1])

    own = pl.BlockSpec(
        (1, 1, 1, orbitals, orbitals), lambda p, j, place, *_: (1 - energy_of(j, place), 0, p, 0, 0)
    )
    arrived = pl.BlockSpec((2, 1, orbitals, orbitals), lambda p, j, *_: (0, p, 0, 0))
    corner = pl.BlockSpec(
        (1, 2, 1, width, width), lambda p, j, place, *_: (energy_of(j, place), 0, p, 0, 0)
    )
    out = pl.BlockSpec((1, 1, orbitals, orbitals), lambda p, j, *_: (j, p, 0, 0))
    return pl.pallas_call(
        near_kernel,
        grid_spec=pltpu.PrefetchScalarGridSpec(
            num_scalar_prefetch=4,
            grid=(parts, 2),
            in_specs=[own, own, arrived, arrived, corner, corner]
            + [
                pl.BlockSpec((1, modes, orbitals, orbitals), lambda p, j, *_: (0, 0, 0, 0)),
                pl.BlockSpec((1, 2, width, width), lambda p, j, *_: (0, 0, 0, 0)),
            ],
            out_specs=[out, out],
            scratch_shapes=[pltpu.VMEM((2, orbitals, orbitals), jnp.float32)],
        ),
        out_shape=[jax.ShapeDtypeStruct((2, parts, orbitals, orbitals), jnp.float32)] * 2,
        compiler_params=pltpu.CompilerParams(vmem_limit_bytes=32 * 2**20),
        cost_estimate=pl.CostEstimate(
            flops=parts * 4 * modes * 4 * orbitals**3, bytes_accessed=20 * 2**20, transcendentals=0
        ),
        name="near_terms",
    )(*scalars, bose, lesser, greater, *near, *corners, couplings, rim_couple)


def bulk_kernel(place, low, ret, low_first, low_second, ret_first, ret_second, low_out, ret_out):
    core = place[1]
    low_out[core, 0, 0] = (low[0, 0] + low_first[...].astype(jnp.float32)).astype(jnp.bfloat16)
    low_out[1 - core, 0, 0] = (low[1, 0] + low_second[...].astype(jnp.float32)).astype(jnp.bfloat16)

    @pl.when(pl.program_id(0) < pl.num_programs(0) - 1)
    def _():
        ret_out[core, 0, 0] = (ret[0, 0] + ret_first[...].astype(jnp.float32)).astype(jnp.bfloat16)
        ret_out[1 - core, 0, 0] = (ret[1, 0] + ret_second[...].astype(jnp.float32)).astype(jnp.bfloat16)


def bulk_added(place, low, ret, far_first, far_second):
    parts, orbitals = low.shape[1], low.shape[-1]
    rows = orbitals // 2
    steps = 2 * parts

    def low_at(c):
        return c

    def ret_at(c):
        return jnp.minimum(c, steps - 2)

    def stored(at):
        return pl.BlockSpec((2, 1, rows, orbitals), lambda c, *_: (0, at(c) // 2, at(c) % 2, 0))

    def written(at):
        return pl.BlockSpec(
            (2, 1, 1, rows, orbitals), lambda c, *_: (0, 0, at(c) // 2, at(c) % 2, 0)
        )

    low_far = pl.BlockSpec((rows, orbitals), lambda c, *_: (c, 0))
    ret_far = pl.BlockSpec((rows, orbitals), lambda c, *_: (steps + ret_at(c), 0))
    return pl.pallas_call(
        bulk_kernel,
        grid_spec=pltpu.PrefetchScalarGridSpec(
            num_scalar_prefetch=1,
            grid=(steps,),
            in_specs=[stored(low_at), stored(ret_at), low_far, low_far, ret_far, ret_far],
            out_specs=[written(low_at), written(ret_at)],
        ),
        out_shape=[jax.ShapeDtypeStruct((2, 1, parts, orbitals, orbitals), jnp.bfloat16)] * 2,
        compiler_params=pltpu.CompilerParams(vmem_limit_bytes=20 * 2**20),
        cost_estimate=pl.CostEstimate(
            flops=8 * orbitals**2, bytes_accessed=14 * 2**20, transcendentals=0
        ),
        name="bulk_added",
    )(place, low, ret, far_first, far_second, far_first, far_second)


def rest_kernel(place, ret, first, second, partial, ret_out):
    core = place[1]
    ret_out[core, 0, 0] = (ret[0, 0] + first[...].astype(jnp.float32)).astype(jnp.bfloat16)
    ret_out[1 - core, 0, 0] = (ret[1, 0] + second[...].astype(jnp.float32)).astype(jnp.bfloat16)


def rest_added(place, ret, far_first, far_second, partial):
    parts, orbitals = ret.shape[1], ret.shape[-1]
    rows = far_first.shape[0]
    last = orbitals // rows - 1
    far = pl.BlockSpec((rows, orbitals), lambda i, *_: (0, 0))
    return pl.pallas_call(
        rest_kernel,
        grid_spec=pltpu.PrefetchScalarGridSpec(
            num_scalar_prefetch=1,
            grid=(1,),
            in_specs=[
                pl.BlockSpec((2, 1, rows, orbitals), lambda i, *_: (0, parts - 1, last, 0)),
                far,
                far,
                pl.BlockSpec(memory_space=pl.ANY),
            ],
            out_specs=pl.BlockSpec(
                (2, 1, 1, rows, orbitals), lambda i, *_: (0, 0, parts - 1, last, 0)
            ),
        ),
        out_shape=jax.ShapeDtypeStruct(partial.shape, partial.dtype),
        input_output_aliases={4: 0},
        compiler_params=pltpu.CompilerParams(vmem_limit_bytes=12 * 2**20),
        cost_estimate=pl.CostEstimate(
            flops=orbitals**2, bytes_accessed=2 * 2**20, transcendentals=0
        ),
        name="rest_added",
    )(place, ret, far_first, far_second, partial)


def body(lesser, greater, couplings, rim_couple, bose_factor, offsets, pattern):
    energies = lax.axis_size("energy")
    cuts = lax.axis_size("cuts")
    orbitals = lesser.shape[-1]
    width = rim_couple.shape[-1]
    cut = lax.axis_index("cuts")
    core = cut & 1
    place = jnp.stack([cut, core]).astype(jnp.int32)
    scalars = (place, offsets, pattern)

    parts = lesser.shape[2]
    whole = (2, parts, orbitals, orbitals)
    corner = (2, 2, parts, width, width)
    cornering = functools.partial(corner_kernel, width)
    inner, outer = copied(cornering, [corner, corner], 4, place, lesser, greater)
    outer = swapped(outer, energies, cuts, False)
    near = []
    for first in (True, False):
        taking = functools.partial(near_copy_kernel, first)
        sent = copied(taking, [whole], 2, place, lesser, greater)[0]
        near.append(shifted(sent, energies, cuts, first))
    inner = swapped(inner, energies, cuts, True)

    bulk, rest = [], []
    outer, place_first = lax.optimization_barrier((outer, place))
    most, last = far_terms(0, (place_first, offsets, pattern), bose_factor, lesser, greater, couplings)
    bulk.append(shifted(most, energies, cuts, True))
    inner, place_second, last = lax.optimization_barrier((inner, place_first, last))
    rest.append(last)
    most, last = far_terms(1, (place_second, offsets, pattern), bose_factor, lesser, greater, couplings)
    bulk.append(shifted(most, energies, cuts, False))
    rest.append(last)
    near[0], near[1], rest[0], rest[1] = lax.optimization_barrier((*near, *rest))
    rest = [shifted(last, energies, cuts, slot == 0) for slot, last in enumerate(rest)]

    low, ret = near_terms(
        scalars, bose_factor, lesser, greater, near, (inner, outer), couplings, rim_couple
    )
    low_out, partial = bulk_added(place, low, ret, *bulk)
    return low_out, rest_added(place, ret, *rest, partial)


def solution(mesh):
    return jax.shard_map(
        body,
        mesh=mesh,
        in_specs=(
            P("energy", "cuts", None, None, None),
            P("energy", "cuts", None, None, None),
            P("cuts", None, None, None),
            P("cuts", None, None, None),
            P(),
            P(),
            P(),
        ),
        out_specs=(P("energy", "cuts", None, None, None), P("energy", "cuts", None, None, None)),
        check_vma=False,
    )
```

```python
import jax
import jax.numpy as jnp
from jax import lax
from jax.experimental import pallas as pl
from jax.experimental.pallas import tpu as pltpu
from jax.sharding import PartitionSpec as P


def shifted(x, energies, cuts, first):
    pairs = []
    for e in range(energies):
        for c in range(cuts):
            up = (c % 2 == 0) == first
            to = e + 1 if up else e - 1
            if 0 <= to < energies:
                pairs.append((e * cuts + c, to * cuts + c))
    return lax.ppermute(x, ("energy", "cuts"), pairs)


def swapped(x, energies, cuts, inside):
    pairs = []
    for e in range(energies):
        for c in range(cuts):
            to = c ^ 1 if inside else (c + 1 if c % 2 else c - 1)
            if 0 <= to < cuts:
                pairs.append((e * cuts + c, e * cuts + to))
    return lax.ppermute(x, ("energy", "cuts"), pairs)


def product(a, b):
    return lax.dot_general(a, b, (((1,), (0,)), ((), ())), preferred_element_type=jnp.float32)


def product_t(a, b):
    return lax.dot_general(a, b, (((1,), (1,)), ((), ())), preferred_element_type=jnp.float32)


def call(kernel, name, scalars, operands, grid, in_specs, out_specs, out_shape, vmem, flops, **more):
    scratch = more.pop("scratch", [])
    return pl.pallas_call(
        kernel,
        grid_spec=pltpu.PrefetchScalarGridSpec(
            num_scalar_prefetch=len(scalars),
            grid=grid,
            in_specs=in_specs,
            out_specs=out_specs,
            scratch_shapes=scratch,
        ),
        out_shape=out_shape,
        compiler_params=pltpu.CompilerParams(vmem_limit_bytes=vmem * 2**20),
        cost_estimate=pl.CostEstimate(flops=flops, bytes_accessed=4 * 2**20, transcendentals=0),
        name=name,
        **more,
    )(*scalars, *operands)


def corner_kernel(place, low_top, high_top, low_bottom, high_bottom, top_out, bottom_out):
    for kind, (top, bottom) in enumerate(((low_top, low_bottom), (high_top, high_bottom))):
        top_out[:, kind] = top[:, 0]
        bottom_out[:, kind] = bottom[:, 0]


def cornered(width, place, lesser, greater):
    parts = lesser.shape[2]
    last = lesser.shape[-1] // width - 1
    shape = (2, 2, parts, width, width)
    block = (2, 1, parts, width, width)

    def outer_at(i, place):
        return (0, 0, 0, place[1] * last, place[1] * last)

    def inner_at(i, place):
        return (0, 0, 0, (1 - place[1]) * last, (1 - place[1]) * last)

    return call(
        corner_kernel,
        "cornered",
        (place,),
        (lesser, greater, lesser, greater),
        (1,),
        [pl.BlockSpec(block, inner_at)] * 2 + [pl.BlockSpec(block, outer_at)] * 2,
        [pl.BlockSpec(shape, lambda i, *_: (0, 0, 0, 0, 0))] * 2,
        [jax.ShapeDtypeStruct(shape, lesser.dtype)] * 2,
        60,
        0,
    )


def pack_kernel(place, green, out):
    out[0] = green[0, 0, 0]


def packed(first, place, greater):
    orbitals = greater.shape[-1]

    def taken(s, place):
        near = 1 - place[1] if first else place[1]
        return (jnp.where(s < 2, s, near), 0, jnp.where(s < 2, 0, 1), 0, 0)

    return call(
        pack_kernel,
        "packed",
        (place,),
        (greater,),
        (3,),
        [pl.BlockSpec((1, 1, 1, orbitals, orbitals), taken)],
        pl.BlockSpec((1, orbitals, orbitals), lambda s, *_: (s, 0, 0)),
        jax.ShapeDtypeStruct((3, orbitals, orbitals), greater.dtype),
        60,
        0,
    )


def far_kernel(place, offsets, pattern, bose, green, couple, first_out, second_out, total):
    cut, core = place[0], place[1]
    slot = pl.program_id(0)
    energy = jnp.where(slot == 0, core, 1 - core)
    total[...] = jnp.zeros_like(total)
    for mode in range(couple.shape[1]):

        @pl.when((pattern[cut, mode] > 0) & (offsets[mode] == 2))
        def _():
            matrix = couple[0, mode]
            weight = bose[mode] + jnp.where(energy == 0, 1.0, 0.0)
            left = (product(matrix, green[0, 0, 0]) * weight).astype(jnp.bfloat16)
            total[...] += product_t(left, matrix)

    for at, out in enumerate((first_out, second_out)):

        @pl.when(slot == at)
        def _():
            out[...] = (0.5 * total[...]).astype(jnp.bfloat16)


def far_terms(scalars, bose, greater, couplings):
    orbitals = greater.shape[-1]
    modes = couplings.shape[1]

    def green_at(j, place, *_):
        return (jnp.where(j == 0, place[1], 1 - place[1]), 0, 1, 0, 0)

    whole = pl.BlockSpec((orbitals, orbitals), lambda j, *_: (0, 0))
    return call(
        far_kernel,
        "far_terms",
        (*scalars, bose),
        (greater, couplings),
        (2,),
        [
            pl.BlockSpec((1, 1, 1, orbitals, orbitals), green_at),
            pl.BlockSpec((1, modes, orbitals, orbitals), lambda j, *_: (0, 0, 0, 0)),
        ],
        [whole, whole],
        [jax.ShapeDtypeStruct((orbitals, orbitals), jnp.bfloat16)] * 2,
        32,
        2 * modes * 16 * orbitals**3,
        scratch=[pltpu.VMEM((orbitals, orbitals), jnp.float32)],
    )


def fetch(pairs, sems):
    copies = [pltpu.make_async_copy(src, dst, sems.at[i]) for i, (src, dst) in enumerate(pairs)]
    for copy in copies:
        copy.start()
    for copy in copies:
        copy.wait()


def mode_sum(kind, energy, cut, offsets, pattern, bose, window, couple, total):
    total[...] = jnp.zeros_like(total)
    for mode in range(couple.shape[1]):

        @pl.when(pattern[cut, mode] > 0)
        def _():
            shift = offsets[mode]
            lead = bose[mode] + (1.0 if kind == 0 else 0.0)
            trail = bose[mode] + (0.0 if kind == 0 else 1.0)
            mixed = (
                lead * window[2 + energy + shift].astype(jnp.float32)
                + trail * window[2 + energy - shift].astype(jnp.float32)
            ).astype(jnp.bfloat16)
            matrix = couple[0, mode]
            left = product(matrix, mixed).astype(jnp.bfloat16)
            total[...] += product_t(left, matrix)


def add_corners(core, inner, outer, rim, total):
    orbitals, width = total.shape[-1], rim.shape[-1]
    for side in range(2):
        matrix = rim[0, side]
        corner = jnp.where(core == side, outer[0, 0, 0], inner[0, 0, 0])
        left = product(matrix, corner).astype(jnp.bfloat16)
        at = slice(0, width) if side == 0 else slice(orbitals - width, orbitals)
        total[at, at] += product_t(left, matrix)


def lesser_kernel(
    place, offsets, pattern, bose,
    own, first, second, inner, outer, couple, rim, out, kept, window, total, sems,
):
    cut, core = place[0], place[1]
    part, energy = pl.program_id(0), pl.program_id(1)

    @pl.when((part == 0) & (energy == 0))
    def _():
        pairs = []
        for p in range(2):
            pairs += [
                (own.at[:, 0, p], window.at[p, pl.ds(2, 2)]),
                (first.at[:, 0, p], window.at[p, pl.ds(4 * core, 2)]),
                (second.at[:, 0, p], window.at[p, pl.ds(4 - 4 * core, 2)]),
            ]
        fetch(pairs, sems)

    mode_sum(0, energy, cut, offsets, pattern, bose, window.at[part], couple, total)
    add_corners(core, inner, outer, rim, total)
    out[0, 0, 0] = total[...].astype(jnp.bfloat16)
    kept[0, 0] = total[...]


def greater_kernel(
    place, offsets, pattern, bose,
    own, first, second, inner, outer, low, couple, rim, out, kept, window, total, sems,
):
    cut, core = place[0], place[1]
    part, energy = pl.program_id(0), pl.program_id(1)

    @pl.when((part == 0) & (energy == 0))
    def _():
        pairs = [(own.at[:, 0, p], window.at[p, pl.ds(2, 2)]) for p in range(2)]
        pairs += [
            (first.at[pl.ds(0, 2)], window.at[0, pl.ds(4 * core, 2)]),
            (second.at[pl.ds(0, 2)], window.at[0, pl.ds(4 - 4 * core, 2)]),
            (first.at[2], window.at[1, 1 + 3 * core]),
            (second.at[2], window.at[1, 4 - 3 * core]),
        ]
        window[1, 0] = jnp.zeros(window.shape[2:], window.dtype)
        window[1, 5] = jnp.zeros(window.shape[2:], window.dtype)
        fetch(pairs, sems)

    mode_sum(1, energy, cut, offsets, pattern, bose, window.at[part], couple, total)
    add_corners(core, inner, outer, rim, total)
    retarded = 0.5 * (total[...] - low[0, 0])

    @pl.when(part == 0)
    def _():
        out[energy, 0, 0] = retarded.astype(jnp.bfloat16)

    @pl.when(part == 1)
    def _():
        kept[energy] = retarded


def product_specs(kind, couplings, rim_couple):
    modes, orbitals = couplings.shape[1], couplings.shape[2]
    width = rim_couple.shape[-1]
    corner = pl.BlockSpec((1, 1, 1, width, width), lambda p, e, *_: (e, kind, p, 0, 0))
    matrices = [
        pl.BlockSpec((1, modes, orbitals, orbitals), lambda p, e, *_: (0, 0, 0, 0)),
        pl.BlockSpec((1, 2, width, width), lambda p, e, *_: (0, 0, 0, 0)),
    ]
    scratch = [
        pltpu.VMEM((2, 6, orbitals, orbitals), jnp.bfloat16),
        pltpu.VMEM((orbitals, orbitals), jnp.float32),
        pltpu.SemaphoreType.DMA((6,)),
    ]
    return [pl.BlockSpec(memory_space=pl.ANY)] * 3 + [corner, corner], matrices, scratch


def lesser_terms(scalars, bose, lesser, first, second, corners, couplings, rim_couple):
    parts, orbitals = lesser.shape[2], lesser.shape[-1]
    inputs, matrices, scratch = product_specs(0, couplings, rim_couple)
    return call(
        lesser_kernel,
        "lesser_terms",
        (*scalars, bose),
        (lesser, first, second, *corners, couplings, rim_couple),
        (parts, 2),
        inputs + matrices,
        [
            pl.BlockSpec((1, 1, 1, orbitals, orbitals), lambda p, e, *_: (e, 0, p, 0, 0)),
            pl.BlockSpec((1, 1, orbitals, orbitals), lambda p, e, *_: (p, e, 0, 0)),
        ],
        [
            jax.ShapeDtypeStruct(lesser.shape, jnp.bfloat16),
            jax.ShapeDtypeStruct((parts, 2, orbitals, orbitals), jnp.float32),
        ],
        60,
        12 * 8 * orbitals**3,
        scratch=scratch,
    )


def greater_terms(scalars, bose, greater, first, second, corners, low, couplings, rim_couple):
    parts, orbitals = greater.shape[2], greater.shape[-1]
    inputs, matrices, scratch = product_specs(1, couplings, rim_couple)
    kept = pl.BlockSpec((1, 1, orbitals, orbitals), lambda p, e, *_: (p, e, 0, 0))
    return call(
        greater_kernel,
        "greater_terms",
        (*scalars, bose),
        (greater, first, second, *corners, low, couplings, rim_couple),
        (parts, 2),
        inputs + [kept] + matrices,
        [
            pl.BlockSpec((2, 1, 1, orbitals, orbitals), lambda p, e, *_: (0, 0, 0, 0, 0)),
            pl.BlockSpec((2, orbitals, orbitals), lambda p, e, *_: (0, 0, 0)),
        ],
        [
            jax.ShapeDtypeStruct(greater.shape, jnp.bfloat16),
            jax.ShapeDtypeStruct((2, orbitals, orbitals), jnp.float32),
        ],
        60,
        12 * 8 * orbitals**3,
        scratch=scratch,
    )


def add_kernel(place, near, first, second, partial, out):
    core = place[1]
    out[core, 0, 0] = (near[core] + first[...].astype(jnp.float32)).astype(out.dtype)
    out[1 - core, 0, 0] = (near[1 - core] + second[...].astype(jnp.float32)).astype(out.dtype)


def added(place, near, far_first, far_second, partial):
    parts, orbitals = partial.shape[2], partial.shape[-1]
    rows = orbitals // 2
    far = pl.BlockSpec((rows, orbitals), lambda r, *_: (r, 0))
    return call(
        add_kernel,
        "added",
        (place,),
        (near, far_first, far_second, partial),
        (orbitals // rows,),
        [
            pl.BlockSpec((2, rows, orbitals), lambda r, *_: (0, r, 0)),
            far,
            far,
            pl.BlockSpec(memory_space=pl.ANY),
        ],
        pl.BlockSpec((2, 1, 1, rows, orbitals), lambda r, *_: (0, 0, parts - 1, r, 0)),
        jax.ShapeDtypeStruct(partial.shape, partial.dtype),
        16,
        orbitals**2,
        input_output_aliases={4: 0},
    )


def body(lesser, greater, couplings, rim_couple, bose_factor, offsets, pattern):
    energies = lax.axis_size("energy")
    cuts = lax.axis_size("cuts")
    width = rim_couple.shape[-1]
    cut = lax.axis_index("cuts")
    place = jnp.stack([cut, cut & 1]).astype(jnp.int32)
    scalars = (place, offsets, pattern)

    low = [shifted(lesser, energies, cuts, first) for first in (True, False)]
    high = [shifted(packed(first, place, greater), energies, cuts, first) for first in (True, False)]
    inner, outer = cornered(width, place, lesser, greater)
    inner = swapped(inner, energies, cuts, True)
    inner, outer = lax.optimization_barrier((inner, outer))
    outer = swapped(outer, energies, cuts, False)
    corners = (inner, outer)

    far = list(far_terms(scalars, bose_factor, greater, couplings))
    low[0], low[1], far[0], far[1] = lax.optimization_barrier((*low, *far))
    far = [shifted(term, energies, cuts, slot == 0) for slot, term in enumerate(far)]

    low_out, low_kept = lesser_terms(
        scalars, bose_factor, lesser, *low, corners, couplings, rim_couple
    )
    partial, near = greater_terms(
        scalars, bose_factor, greater, *high, corners, low_kept, couplings, rim_couple
    )
    return low_out, added(place, near, *far, partial)


def solution(mesh):
    return jax.shard_map(
        body,
        mesh=mesh,
        in_specs=(
            P("energy", "cuts", None, None, None),
            P("energy", "cuts", None, None, None),
            P("cuts", None, None, None),
            P("cuts", None, None, None),
            P(),
            P(),
            P(),
        ),
        out_specs=(P("energy", "cuts", None, None, None), P("energy", "cuts", None, None, None)),
        check_vma=False,
    )
```

```python
import jax
import jax.numpy as jnp
from jax import lax
from jax.experimental import pallas as pl
from jax.experimental.pallas import tpu as pltpu
from jax.sharding import PartitionSpec as P


def shifted(x, energies, cuts, first):
    pairs = []
    for e in range(energies):
        for c in range(cuts):
            up = (c % 2 == 0) == first
            to = e + 1 if up else e - 1
            if 0 <= to < energies:
                pairs.append((e * cuts + c, to * cuts + c))
    return lax.ppermute(x, ("energy", "cuts"), pairs)


def swapped(x, energies, cuts, inside):
    pairs = []
    for e in range(energies):
        for c in range(cuts):
            to = c ^ 1 if inside else (c + 1 if c % 2 else c - 1)
            if 0 <= to < cuts:
                pairs.append((e * cuts + c, e * cuts + to))
    return lax.ppermute(x, ("energy", "cuts"), pairs)


def product(a, b):
    return lax.dot_general(a, b, (((1,), (0,)), ((), ())), preferred_element_type=jnp.float32)


def product_t(a, b):
    return lax.dot_general(a, b, (((1,), (1,)), ((), ())), preferred_element_type=jnp.float32)


def call(kernel, name, scalars, operands, grid, in_specs, out_specs, out_shape, vmem, flops, **more):
    scratch = more.pop("scratch", [])
    return pl.pallas_call(
        kernel,
        grid_spec=pltpu.PrefetchScalarGridSpec(
            num_scalar_prefetch=len(scalars),
            grid=grid,
            in_specs=in_specs,
            out_specs=out_specs,
            scratch_shapes=scratch,
        ),
        out_shape=out_shape,
        compiler_params=pltpu.CompilerParams(vmem_limit_bytes=vmem * 2**20),
        cost_estimate=pl.CostEstimate(flops=flops, bytes_accessed=4 * 2**20, transcendentals=0),
        name=name,
        **more,
    )(*scalars, *operands)


def corner_kernel(inside, low_top, high_top, low_bottom, high_bottom, out):
    core = lax.axis_index("cuts") & 1
    for kind, (top, bottom) in enumerate(((low_top, low_bottom), (high_top, high_bottom))):
        upper = core == 1 if inside else core == 0
        out[:, kind] = jnp.where(upper, top[:, 0], bottom[:, 0])


def cornered(inside, width, lesser, greater):
    parts = lesser.shape[2]
    last = lesser.shape[-1] // width - 1
    shape = (2, 2, parts, width, width)
    block = (2, 1, parts, width, width)
    top = pl.BlockSpec(block, lambda i: (0, 0, 0, 0, 0))
    bottom = pl.BlockSpec(block, lambda i: (0, 0, 0, last, last))
    return call(
        lambda *refs: corner_kernel(inside, *refs),
        "cornered",
        (),
        (lesser, greater, lesser, greater),
        (1,),
        [top, top, bottom, bottom],
        pl.BlockSpec(shape, lambda i: (0, 0, 0, 0, 0)),
        jax.ShapeDtypeStruct(shape, lesser.dtype),
        60,
        0,
    )


def place_kernel(out):
    cut = lax.axis_index("cuts")
    out[0] = cut
    out[1] = cut & 1


def placed():
    return call(
        place_kernel,
        "placed",
        (),
        (),
        (),
        [],
        pl.BlockSpec(memory_space=pltpu.SMEM),
        jax.ShapeDtypeStruct((2,), jnp.int32),
        60,
        10**12,
    )


def far_kernel(place, offsets, pattern, bose, green, couple, first_out, second_out, left, total):
    cut, core = place[0], place[1]
    orbitals = couple.shape[-1]
    total[...] = jnp.zeros_like(total)
    for mode in range(couple.shape[1]):

        @pl.when((pattern[cut, mode] > 0) & (offsets[mode] == 2))
        def _():
            matrix = couple[0, mode]
            for energy in range(2):
                weight = bose[mode] + (1.0 if energy == 0 else 0.0)
                rows = slice(energy * orbitals, (energy + 1) * orbitals)
                left[rows] = (product(matrix, green[energy, 0, 0]) * weight).astype(jnp.bfloat16)
            total[...] += product_t(left[...], matrix)

    for slot, out in enumerate((first_out, second_out)):
        start = pl.multiple_of((core if slot == 0 else 1 - core) * orbitals, orbitals)
        out[0] = (0.5 * total[pl.ds(start, orbitals)]).astype(jnp.bfloat16)


def far_terms(scalars, bose, greater, couplings):
    parts, orbitals = greater.shape[2], greater.shape[-1]
    modes = couplings.shape[1]
    whole = pl.BlockSpec((1, orbitals, orbitals), lambda p, *_: (p, 0, 0))
    return call(
        far_kernel,
        "far_terms",
        (*scalars, bose),
        (greater, couplings),
        (parts,),
        [
            pl.BlockSpec((2, 1, 1, orbitals, orbitals), lambda p, *_: (0, 0, p, 0, 0)),
            pl.BlockSpec((1, modes, orbitals, orbitals), lambda p, *_: (0, 0, 0, 0)),
        ],
        [whole, whole],
        [jax.ShapeDtypeStruct((parts, orbitals, orbitals), jnp.bfloat16)] * 2,
        60,
        64 * modes * orbitals**3,
        scratch=[
            pltpu.VMEM((2 * orbitals, orbitals), jnp.bfloat16),
            pltpu.VMEM((2 * orbitals, orbitals), jnp.float32),
        ],
    )


def fetch(part, parts, copies):
    @pl.when(part == 0)
    def _():
        for copy in sum(copies, []):
            copy.start()

    for p in range(parts):

        @pl.when(part == p)
        def _():
            for copy in copies[p]:
                copy.wait()


def add_corners(core, inner, outer, rim, total):
    orbitals, width = total.shape[-1], rim.shape[-1]
    for energy in range(2):
        for side in range(2):
            matrix = rim[0, side]
            corner = jnp.where(core == side, outer[energy, 0, 0], inner[energy, 0, 0])
            left = product(matrix, corner).astype(jnp.bfloat16)
            start = 0 if side == 0 else orbitals - width
            rows = slice(energy * orbitals + start, energy * orbitals + start + width)
            total[rows, start : start + width] += product_t(left, matrix)


def blended(ahead, lead, behind, trail):
    mixed = lead * ahead.astype(jnp.float32) + trail * behind.astype(jnp.float32)
    return mixed.astype(jnp.bfloat16)


def lesser_kernel(
    place, offsets, pattern, bose,
    own, first, second, inner, outer, couple, rim, out, kept, window, left, total, sems,
):
    cut, core = place[0], place[1]
    part = pl.program_id(0)
    orbitals = couple.shape[-1]
    fetch(
        part,
        2,
        [
            [
                pltpu.make_async_copy(own.at[:, 0, p], window.at[p, pl.ds(2, 2)], sems.at[p, 0]),
                pltpu.make_async_copy(
                    first.at[:, 0, p], window.at[p, pl.ds(4 * core, 2)], sems.at[p, 1]
                ),
                pltpu.make_async_copy(
                    second.at[:, 0, p], window.at[p, pl.ds(4 - 4 * core, 2)], sems.at[p, 2]
                ),
            ]
            for p in range(2)
        ],
    )
    here = window.at[part]
    total[...] = jnp.zeros_like(total)
    add_corners(core, inner, outer, rim, total)
    for mode in range(couple.shape[1]):

        @pl.when(pattern[cut, mode] > 0)
        def _():
            shift, matrix = offsets[mode], couple[0, mode]
            for energy in range(2):
                rows = slice(energy * orbitals, (energy + 1) * orbitals)
                mixed = blended(
                    here[2 + energy + shift], bose[mode] + 1.0, here[2 + energy - shift], bose[mode]
                )
                left[rows] = product(matrix, mixed).astype(jnp.bfloat16)
            total[...] += product_t(left[...], matrix)

    for energy in range(2):
        rows = slice(energy * orbitals, (energy + 1) * orbitals)
        out[energy, 0, 0] = total[rows].astype(jnp.bfloat16)
        kept[0, energy] = total[rows]


def greater_kernel(
    place, offsets, pattern, bose,
    own, first, second, inner, outer, low, couple, rim, kept, window, left, total, sems,
):
    cut, core = place[0], place[1]
    part = pl.program_id(0)
    orbitals = couple.shape[-1]
    fetch(
        part,
        2,
        [
            [
                pltpu.make_async_copy(own.at[:, 0, p], window.at[p, pl.ds(1, 2)], sems.at[p, 0]),
                pltpu.make_async_copy(first.at[0, 0, p], window.at[p, 3 * core], sems.at[p, 1]),
                pltpu.make_async_copy(second.at[0, 0, p], window.at[p, 3 - 3 * core], sems.at[p, 2]),
            ]
            for p in range(2)
        ],
    )
    here = window.at[part]
    total[...] = jnp.zeros_like(total)
    add_corners(core, inner, outer, rim, total)
    for mode in range(couple.shape[1]):
        active = pattern[cut, mode] > 0

        @pl.when(active & (offsets[mode] == 2))
        def _():
            matrix = couple[0, mode]
            for energy in range(2):
                rows = slice(energy * orbitals, (energy + 1) * orbitals)
                weight = bose[mode] + (0.0 if energy == 0 else 1.0)
                left[rows] = (product(matrix, here[3 - 3 * energy]) * weight).astype(jnp.bfloat16)
            total[...] += product_t(left[...], matrix)

        @pl.when(active & (offsets[mode] != 2))
        def _():
            matrix = couple[0, mode]
            for energy in range(2):
                rows = slice(energy * orbitals, (energy + 1) * orbitals)
                mixed = blended(here[2 + energy], bose[mode], here[energy], bose[mode] + 1.0)
                left[rows] = product(matrix, mixed).astype(jnp.bfloat16)
            total[...] += product_t(left[...], matrix)

    for energy in range(2):
        rows = slice(energy * orbitals, (energy + 1) * orbitals)
        kept[energy, 0, 0] = (0.5 * (total[rows] - low[0, energy])).astype(kept.dtype)


def product_specs(kind, slots, couplings, rim_couple):
    modes, orbitals = couplings.shape[1], couplings.shape[2]
    width = rim_couple.shape[-1]
    corner = pl.BlockSpec((2, 1, 1, width, width), lambda p, *_: (0, kind, p, 0, 0))
    matrices = [
        pl.BlockSpec((1, modes, orbitals, orbitals), lambda p, *_: (0, 0, 0, 0)),
        pl.BlockSpec((1, 2, width, width), lambda p, *_: (0, 0, 0, 0)),
    ]
    scratch = [
        pltpu.VMEM((2, slots, orbitals, orbitals), jnp.bfloat16),
        pltpu.VMEM((2 * orbitals, orbitals), jnp.bfloat16),
        pltpu.VMEM((2 * orbitals, orbitals), jnp.float32),
        pltpu.SemaphoreType.DMA((2, 3)),
    ]
    kept = pl.BlockSpec((1, 2, orbitals, orbitals), lambda p, *_: (p, 0, 0, 0))
    return [pl.BlockSpec(memory_space=pl.ANY)] * 3 + [corner, corner], matrices, kept, scratch


def lesser_terms(scalars, bose, lesser, first, second, corners, couplings, rim_couple):
    parts, orbitals = lesser.shape[2], lesser.shape[-1]
    inputs, matrices, kept, scratch = product_specs(0, 6, couplings, rim_couple)
    return call(
        lesser_kernel,
        "lesser_terms",
        (*scalars, bose),
        (lesser, first, second, *corners, couplings, rim_couple),
        (parts,),
        inputs + matrices,
        [pl.BlockSpec((2, 1, 1, orbitals, orbitals), lambda p, *_: (0, 0, p, 0, 0)), kept],
        [
            jax.ShapeDtypeStruct(lesser.shape, jnp.bfloat16),
            jax.ShapeDtypeStruct((parts, 2, orbitals, orbitals), jnp.float32),
        ],
        60,
        12 * 8 * orbitals**3,
        scratch=scratch,
    )


def greater_terms(scalars, bose, greater, first, second, corners, low, couplings, rim_couple):
    parts, orbitals = greater.shape[2], greater.shape[-1]
    inputs, matrices, kept, scratch = product_specs(1, 4, couplings, rim_couple)
    return call(
        greater_kernel,
        "greater_terms",
        (*scalars, bose),
        (greater, first, second, *corners, low, couplings, rim_couple),
        (parts,),
        inputs + [kept] + matrices,
        pl.BlockSpec((2, 1, 1, orbitals, orbitals), lambda p, *_: (0, 0, p, 0, 0)),
        jax.ShapeDtypeStruct(greater.shape, jnp.bfloat16),
        60,
        12 * 8 * orbitals**3,
        scratch=scratch,
    )


def added(core, near, first, second):
    energy = lax.broadcasted_iota(jnp.int32, near.shape, 0)
    far = jnp.where(energy == core, first[None, None], second[None, None])
    return (near.astype(jnp.float32) + far.astype(jnp.float32)).astype(jnp.bfloat16)


def body(lesser, greater, couplings, rim_couple, bose_factor, offsets, pattern):
    energies = lax.axis_size("energy")
    cuts = lax.axis_size("cuts")
    width = rim_couple.shape[-1]
    core = lax.axis_index("cuts") & 1

    outer = swapped(cornered(False, width, lesser, greater), energies, cuts, False)
    place, lesser_sent = lax.optimization_barrier((placed(), lesser))
    low = [shifted(lesser_sent, energies, cuts, first) for first in (True, False)]
    near = [lax.dynamic_slice_in_dim(greater, at, 1, 0) for at in (1 - core, core)]
    outer, place = lax.optimization_barrier((outer, place))
    high = [shifted(term, energies, cuts, i == 0) for i, term in enumerate(near)]
    scalars = (place, offsets, pattern)

    first, second = far_terms(scalars, bose_factor, greater, couplings)
    second, lesser_corner = lax.optimization_barrier((second, lesser))
    inner = swapped(cornered(True, width, lesser_corner, greater), energies, cuts, True)
    inner, first = lax.optimization_barrier((inner, first))
    corners = (inner, outer)
    first = shifted(first, energies, cuts, True)
    low, second = lax.optimization_barrier((low, second))
    second = shifted(second, energies, cuts, False)

    low_out, low_kept = lesser_terms(
        scalars, bose_factor, lesser, *low, corners, couplings, rim_couple
    )
    kept = greater_terms(
        scalars, bose_factor, greater, *high, corners, low_kept, couplings, rim_couple
    )
    return low_out, added(core, kept, first, second)


def solution(mesh):
    return jax.shard_map(
        body,
        mesh=mesh,
        in_specs=(
            P("energy", "cuts", None, None, None),
            P("energy", "cuts", None, None, None),
            P("cuts", None, None, None),
            P("cuts", None, None, None),
            P(),
            P(),
            P(),
        ),
        out_specs=(P("energy", "cuts", None, None, None), P("energy", "cuts", None, None, None)),
        check_vma=False,
    )
```

```python
import jax
import jax.numpy as jnp
from jax import lax
from jax.experimental import pallas as pl
from jax.experimental.pallas import tpu as pltpu
from jax.sharding import PartitionSpec as P


def shifted(x, energies, cuts, first):
    pairs = []
    for e in range(energies):
        for c in range(cuts):
            up = (c % 2 == 0) == first
            to = e + 1 if up else e - 1
            if 0 <= to < energies:
                pairs.append((e * cuts + c, to * cuts + c))
    return lax.ppermute(x, ("energy", "cuts"), pairs)


def swapped(x, energies, cuts, inside):
    pairs = []
    for e in range(energies):
        for c in range(cuts):
            to = c ^ 1 if inside else (c + 1 if c % 2 else c - 1)
            if 0 <= to < cuts:
                pairs.append((e * cuts + c, e * cuts + to))
    return lax.ppermute(x, ("energy", "cuts"), pairs)


def product(a, b):
    return lax.dot_general(a, b, (((1,), (0,)), ((), ())), preferred_element_type=jnp.float32)


def product_t(a, b):
    return lax.dot_general(a, b, (((1,), (1,)), ((), ())), preferred_element_type=jnp.float32)


def call(kernel, name, scalars, operands, grid, in_specs, out_specs, out_shape, vmem, flops, **more):
    scratch = more.pop("scratch", [])
    return pl.pallas_call(
        kernel,
        grid_spec=pltpu.PrefetchScalarGridSpec(
            num_scalar_prefetch=len(scalars),
            grid=grid,
            in_specs=in_specs,
            out_specs=out_specs,
            scratch_shapes=scratch,
        ),
        out_shape=out_shape,
        compiler_params=pltpu.CompilerParams(vmem_limit_bytes=vmem * 2**20),
        cost_estimate=pl.CostEstimate(flops=flops, bytes_accessed=4 * 2**20, transcendentals=0),
        name=name,
        **more,
    )(*scalars, *operands)


def corner_kernel(inside, width, lesser, greater, out, place, sems):
    cut = lax.axis_index("cuts")
    core = cut & 1
    last = (lesser.shape[-1] - width) // width
    upper = (1 - core if inside else core) * last
    edge = pl.ds(pl.multiple_of(upper * width, width), width)
    copies = [
        pltpu.make_async_copy(green.at[:, 0, :, edge, edge], out.at[:, kind], sems.at[kind])
        for kind, green in enumerate((lesser, greater))
    ]
    for copy in copies:
        copy.start()
    place[0] = cut
    place[1] = core
    for copy in copies:
        copy.wait()


def cornered(inside, width, lesser, greater):
    parts = lesser.shape[2]
    shape = (2, 2, parts, width, width)
    anywhere = pl.BlockSpec(memory_space=pl.ANY)
    return call(
        lambda *refs: corner_kernel(inside, width, *refs),
        "cornered",
        (),
        (lesser, greater),
        (1,),
        [anywhere, anywhere],
        [
            pl.BlockSpec(shape, lambda i: (0, 0, 0, 0, 0)),
            pl.BlockSpec(memory_space=pltpu.SMEM),
        ],
        [jax.ShapeDtypeStruct(shape, lesser.dtype), jax.ShapeDtypeStruct((2,), jnp.int32)],
        60,
        0,
        scratch=[pltpu.SemaphoreType.DMA((2,))],
    )


def far_kernel(place, offsets, pattern, bose, green, couple, first_out, second_out, left, total):
    cut, core = place[0], place[1]
    orbitals = couple.shape[-1]
    total[...] = jnp.zeros_like(total)
    for mode in range(couple.shape[1]):

        @pl.when((pattern[cut, mode] > 0) & (offsets[mode] == 2))
        def _():
            matrix = couple[0, mode]
            for energy in range(2):
                weight = bose[mode] + (1.0 if energy == 0 else 0.0)
                rows = slice(energy * orbitals, (energy + 1) * orbitals)
                left[rows] = (product(matrix, green[energy, 0, 0]) * weight).astype(jnp.bfloat16)
            total[...] += product_t(left[...], matrix)

    for slot, out in enumerate((first_out, second_out)):
        start = pl.multiple_of((core if slot == 0 else 1 - core) * orbitals, orbitals)
        out[0] = (0.5 * total[pl.ds(start, orbitals)]).astype(jnp.bfloat16)


def far_terms(scalars, bose, greater, couplings):
    parts, orbitals = greater.shape[2], greater.shape[-1]
    modes = couplings.shape[1]
    whole = pl.BlockSpec((1, orbitals, orbitals), lambda p, *_: (p, 0, 0))
    return call(
        far_kernel,
        "far_terms",
        (*scalars, bose),
        (greater, couplings),
        (parts,),
        [
            pl.BlockSpec((2, 1, 1, orbitals, orbitals), lambda p, *_: (0, 0, p, 0, 0)),
            pl.BlockSpec((1, modes, orbitals, orbitals), lambda p, *_: (0, 0, 0, 0)),
        ],
        [whole, whole],
        [jax.ShapeDtypeStruct((parts, orbitals, orbitals), jnp.bfloat16)] * 2,
        60,
        64 * modes * orbitals**3,
        scratch=[
            pltpu.VMEM((2 * orbitals, orbitals), jnp.bfloat16),
            pltpu.VMEM((2 * orbitals, orbitals), jnp.float32),
        ],
    )


def fetch(part, parts, copies):
    @pl.when(part == 0)
    def _():
        for copy in sum(copies, []):
            copy.start()

    for p in range(parts):

        @pl.when(part == p)
        def _():
            for copy in copies[p]:
                copy.wait()


def add_corners(core, inner, outer, rim, total):
    orbitals, width = total.shape[-1], rim.shape[-1]
    for energy in range(2):
        for side in range(2):
            matrix = rim[0, side]
            corner = jnp.where(core == side, outer[energy, 0, 0], inner[energy, 0, 0])
            left = product(matrix, corner).astype(jnp.bfloat16)
            start = 0 if side == 0 else orbitals - width
            rows = slice(energy * orbitals + start, energy * orbitals + start + width)
            total[rows, start : start + width] += product_t(left, matrix)


def blended(ahead, lead, behind, trail):
    mixed = lead * ahead.astype(jnp.float32) + trail * behind.astype(jnp.float32)
    return mixed.astype(jnp.bfloat16)


def lesser_kernel(
    place, offsets, pattern, bose,
    own, first, second, inner, outer, couple, rim, out, kept, window, left, total, sems,
):
    cut, core = place[0], place[1]
    part = pl.program_id(0)
    orbitals = couple.shape[-1]
    fetch(
        part,
        2,
        [
            [
                pltpu.make_async_copy(own.at[:, 0, p], window.at[p, pl.ds(2, 2)], sems.at[p, 0]),
                pltpu.make_async_copy(
                    first.at[:, 0, p], window.at[p, pl.ds(4 * core, 2)], sems.at[p, 1]
                ),
                pltpu.make_async_copy(
                    second.at[:, 0, p], window.at[p, pl.ds(4 - 4 * core, 2)], sems.at[p, 2]
                ),
            ]
            for p in range(2)
        ],
    )
    here = window.at[part]
    total[...] = jnp.zeros_like(total)
    add_corners(core, inner, outer, rim, total)
    for mode in range(couple.shape[1]):

        @pl.when(pattern[cut, mode] > 0)
        def _():
            shift, matrix = offsets[mode], couple[0, mode]
            for energy in range(2):
                rows = slice(energy * orbitals, (energy + 1) * orbitals)
                mixed = blended(
                    here[2 + energy + shift], bose[mode] + 1.0, here[2 + energy - shift], bose[mode]
                )
                left[rows] = product(matrix, mixed).astype(jnp.bfloat16)
            total[...] += product_t(left[...], matrix)

    for energy in range(2):
        rows = slice(energy * orbitals, (energy + 1) * orbitals)
        out[energy, 0, 0] = total[rows].astype(jnp.bfloat16)
        kept[0, energy] = total[rows]


def greater_kernel(
    place, offsets, pattern, bose,
    own, first, second, inner, outer, low, couple, rim, kept, window, left, total, sems,
):
    cut, core = place[0], place[1]
    part = pl.program_id(0)
    orbitals = couple.shape[-1]
    fetch(
        part,
        2,
        [
            [
                pltpu.make_async_copy(own.at[:, 0, p], window.at[p, pl.ds(1, 2)], sems.at[p, 0]),
                pltpu.make_async_copy(first.at[0, 0, p], window.at[p, 3 * core], sems.at[p, 1]),
                pltpu.make_async_copy(second.at[0, 0, p], window.at[p, 3 - 3 * core], sems.at[p, 2]),
            ]
            for p in range(2)
        ],
    )
    here = window.at[part]
    total[...] = jnp.zeros_like(total)
    add_corners(core, inner, outer, rim, total)
    for mode in range(couple.shape[1]):
        active = pattern[cut, mode] > 0

        @pl.when(active & (offsets[mode] == 2))
        def _():
            matrix = couple[0, mode]
            for energy in range(2):
                rows = slice(energy * orbitals, (energy + 1) * orbitals)
                weight = bose[mode] + (0.0 if energy == 0 else 1.0)
                left[rows] = (product(matrix, here[3 - 3 * energy]) * weight).astype(jnp.bfloat16)
            total[...] += product_t(left[...], matrix)

        @pl.when(active & (offsets[mode] != 2))
        def _():
            matrix = couple[0, mode]
            for energy in range(2):
                rows = slice(energy * orbitals, (energy + 1) * orbitals)
                mixed = blended(here[2 + energy], bose[mode], here[energy], bose[mode] + 1.0)
                left[rows] = product(matrix, mixed).astype(jnp.bfloat16)
            total[...] += product_t(left[...], matrix)

    for energy in range(2):
        rows = slice(energy * orbitals, (energy + 1) * orbitals)
        kept[energy, 0, 0] = (0.5 * (total[rows] - low[0, energy])).astype(kept.dtype)


def product_specs(kind, slots, couplings, rim_couple):
    modes, orbitals = couplings.shape[1], couplings.shape[2]
    width = rim_couple.shape[-1]
    corner = pl.BlockSpec((2, 1, 1, width, width), lambda p, *_: (0, kind, p, 0, 0))
    matrices = [
        pl.BlockSpec((1, modes, orbitals, orbitals), lambda p, *_: (0, 0, 0, 0)),
        pl.BlockSpec((1, 2, width, width), lambda p, *_: (0, 0, 0, 0)),
    ]
    scratch = [
        pltpu.VMEM((2, slots, orbitals, orbitals), jnp.bfloat16),
        pltpu.VMEM((2 * orbitals, orbitals), jnp.bfloat16),
        pltpu.VMEM((2 * orbitals, orbitals), jnp.float32),
        pltpu.SemaphoreType.DMA((2, 3)),
    ]
    kept = pl.BlockSpec((1, 2, orbitals, orbitals), lambda p, *_: (p, 0, 0, 0))
    return [pl.BlockSpec(memory_space=pl.ANY)] * 3 + [corner, corner], matrices, kept, scratch


def lesser_terms(scalars, bose, lesser, first, second, corners, couplings, rim_couple):
    parts, orbitals = lesser.shape[2], lesser.shape[-1]
    inputs, matrices, kept, scratch = product_specs(0, 6, couplings, rim_couple)
    return call(
        lesser_kernel,
        "lesser_terms",
        (*scalars, bose),
        (lesser, first, second, *corners, couplings, rim_couple),
        (parts,),
        inputs + matrices,
        [pl.BlockSpec((2, 1, 1, orbitals, orbitals), lambda p, *_: (0, 0, p, 0, 0)), kept],
        [
            jax.ShapeDtypeStruct(lesser.shape, jnp.bfloat16),
            jax.ShapeDtypeStruct((parts, 2, orbitals, orbitals), jnp.float32),
        ],
        60,
        12 * 8 * orbitals**3,
        scratch=scratch,
    )


def greater_terms(scalars, bose, greater, first, second, corners, low, couplings, rim_couple):
    parts, orbitals = greater.shape[2], greater.shape[-1]
    inputs, matrices, kept, scratch = product_specs(1, 4, couplings, rim_couple)
    return call(
        greater_kernel,
        "greater_terms",
        (*scalars, bose),
        (greater, first, second, *corners, low, couplings, rim_couple),
        (parts,),
        inputs + [kept] + matrices,
        pl.BlockSpec((2, 1, 1, orbitals, orbitals), lambda p, *_: (0, 0, p, 0, 0)),
        jax.ShapeDtypeStruct(greater.shape, jnp.bfloat16),
        60,
        12 * 8 * orbitals**3,
        scratch=scratch,
    )


def add_kernel(place, near, far, out):
    mixed = near[0, 0, 0].astype(jnp.float32) + far[0].astype(jnp.float32)
    out[0, 0, 0] = mixed.astype(out.dtype)


def added(slot, place, near, far):
    parts, orbitals = far.shape[0], far.shape[-1]
    rows = orbitals // 2

    def energy_at(p, r, place):
        return (place[1] if slot == 0 else 1 - place[1], 0, p, r, 0)

    block = pl.BlockSpec((1, 1, 1, rows, orbitals), energy_at)
    return call(
        add_kernel,
        "added",
        (place,),
        (near, far),
        (parts, orbitals // rows),
        [block, pl.BlockSpec((1, rows, orbitals), lambda p, r, *_: (p, r, 0))],
        block,
        jax.ShapeDtypeStruct(near.shape, near.dtype),
        48,
        orbitals**2,
        input_output_aliases={1: 0},
    )


def body(lesser, greater, couplings, rim_couple, bose_factor, offsets, pattern):
    energies = lax.axis_size("energy")
    cuts = lax.axis_size("cuts")
    width = rim_couple.shape[-1]
    core = lax.axis_index("cuts") & 1

    outer, place = cornered(False, width, lesser, greater)
    outer = swapped(outer, energies, cuts, False)
    place, lesser_sent = lax.optimization_barrier((place, lesser))
    low = [shifted(lesser_sent, energies, cuts, first) for first in (True, False)]
    near = [lax.dynamic_slice_in_dim(greater, at, 1, 0) for at in (1 - core, core)]
    outer, place = lax.optimization_barrier((outer, place))
    high = [shifted(term, energies, cuts, i == 0) for i, term in enumerate(near)]
    scalars = (place, offsets, pattern)

    first, second = far_terms(scalars, bose_factor, greater, couplings)
    second, lesser_corner = lax.optimization_barrier((second, lesser))
    inner = swapped(cornered(True, width, lesser_corner, greater)[0], energies, cuts, True)
    inner, first = lax.optimization_barrier((inner, first))
    corners = (inner, outer)
    first = shifted(first, energies, cuts, True)
    low, second = lax.optimization_barrier((low, second))
    second = shifted(second, energies, cuts, False)

    low_out, low_kept = lesser_terms(
        scalars, bose_factor, lesser, *low, corners, couplings, rim_couple
    )
    kept = greater_terms(
        scalars, bose_factor, greater, *high, corners, low_kept, couplings, rim_couple
    )
    return low_out, added(1, place, added(0, place, kept, first), second)


def solution(mesh):
    return jax.shard_map(
        body,
        mesh=mesh,
        in_specs=(
            P("energy", "cuts", None, None, None),
            P("energy", "cuts", None, None, None),
            P("cuts", None, None, None),
            P("cuts", None, None, None),
            P(),
            P(),
            P(),
        ),
        out_specs=(P("energy", "cuts", None, None, None), P("energy", "cuts", None, None, None)),
        check_vma=False,
    )
```

```python
import jax
import jax.numpy as jnp
from jax import lax
from jax.experimental import pallas as pl
from jax.experimental.pallas import tpu as pltpu
from jax.sharding import PartitionSpec as P


def shifted(x, energies, cuts, first):
    pairs = []
    for e in range(energies):
        for c in range(cuts):
            up = (c % 2 == 0) == first
            to = e + 1 if up else e - 1
            if 0 <= to < energies:
                pairs.append((e * cuts + c, to * cuts + c))
    return lax.ppermute(x, ("energy", "cuts"), pairs)


def swapped(x, energies, cuts, inside):
    pairs = []
    for e in range(energies):
        for c in range(cuts):
            to = c ^ 1 if inside else (c + 1 if c % 2 else c - 1)
            if 0 <= to < cuts:
                pairs.append((e * cuts + c, e * cuts + to))
    return lax.ppermute(x, ("energy", "cuts"), pairs)


def product(a, b):
    return lax.dot_general(a, b, (((1,), (0,)), ((), ())), preferred_element_type=jnp.float32)


def product_t(a, b):
    return lax.dot_general(a, b, (((1,), (1,)), ((), ())), preferred_element_type=jnp.float32)


def call(kernel, name, scalars, operands, grid, in_specs, out_specs, out_shape, vmem, flops, **more):
    scratch = more.pop("scratch", [])
    return pl.pallas_call(
        kernel,
        grid_spec=pltpu.PrefetchScalarGridSpec(
            num_scalar_prefetch=len(scalars),
            grid=grid,
            in_specs=in_specs,
            out_specs=out_specs,
            scratch_shapes=scratch,
        ),
        out_shape=out_shape,
        compiler_params=pltpu.CompilerParams(vmem_limit_bytes=vmem * 2**20),
        cost_estimate=pl.CostEstimate(flops=flops, bytes_accessed=4 * 2**20, transcendentals=0),
        name=name,
        **more,
    )(*scalars, *operands)


def corner_kernel(inside, low_top, high_top, low_bottom, high_bottom, out):
    core = lax.axis_index("cuts") & 1
    for kind, (top, bottom) in enumerate(((low_top, low_bottom), (high_top, high_bottom))):
        upper = core == 1 if inside else core == 0
        out[:, kind] = jnp.where(upper, top[:, 0], bottom[:, 0])


def cornered(inside, width, lesser, greater):
    parts = lesser.shape[2]
    last = lesser.shape[-1] // width - 1
    shape = (2, 2, parts, width, width)
    block = (2, 1, parts, width, width)
    top = pl.BlockSpec(block, lambda i: (0, 0, 0, 0, 0))
    bottom = pl.BlockSpec(block, lambda i: (0, 0, 0, last, last))
    return call(
        lambda *refs: corner_kernel(inside, *refs),
        "cornered",
        (),
        (lesser, greater, lesser, greater),
        (1,),
        [top, top, bottom, bottom],
        pl.BlockSpec(shape, lambda i: (0, 0, 0, 0, 0)),
        jax.ShapeDtypeStruct(shape, lesser.dtype),
        60,
        0,
    )


def place_kernel(out):
    cut = lax.axis_index("cuts")
    out[0] = cut
    out[1] = cut & 1


def placed():
    return call(
        place_kernel,
        "placed",
        (),
        (),
        (),
        [],
        pl.BlockSpec(memory_space=pltpu.SMEM),
        jax.ShapeDtypeStruct((2,), jnp.int32),
        60,
        10**12,
    )


def far_kernel(place, offsets, pattern, bose, green, couple, first_out, second_out, left, total):
    cut, core = place[0], place[1]
    orbitals = couple.shape[-1]
    total[...] = jnp.zeros_like(total)
    for mode in range(couple.shape[1]):

        @pl.when((pattern[cut, mode] > 0) & (offsets[mode] == 2))
        def _():
            matrix = couple[0, mode]
            for energy in range(2):
                weight = bose[mode] + (1.0 if energy == 0 else 0.0)
                rows = slice(energy * orbitals, (energy + 1) * orbitals)
                left[rows] = (product(matrix, green[energy, 0, 0]) * weight).astype(jnp.bfloat16)
            total[...] += product_t(left[...], matrix)

    for slot, out in enumerate((first_out, second_out)):
        start = pl.multiple_of((core if slot == 0 else 1 - core) * orbitals, orbitals)
        out[0] = (0.5 * total[pl.ds(start, orbitals)]).astype(jnp.bfloat16)


def far_terms(scalars, bose, greater, couplings):
    parts, orbitals = greater.shape[2], greater.shape[-1]
    modes = couplings.shape[1]
    whole = pl.BlockSpec((1, orbitals, orbitals), lambda p, *_: (p, 0, 0))
    return call(
        far_kernel,
        "far_terms",
        (*scalars, bose),
        (greater, couplings),
        (parts,),
        [
            pl.BlockSpec((2, 1, 1, orbitals, orbitals), lambda p, *_: (0, 0, p, 0, 0)),
            pl.BlockSpec((1, modes, orbitals, orbitals), lambda p, *_: (0, 0, 0, 0)),
        ],
        [whole, whole],
        [jax.ShapeDtypeStruct((parts, orbitals, orbitals), jnp.bfloat16)] * 2,
        60,
        64 * modes * orbitals**3,
        scratch=[
            pltpu.VMEM((2 * orbitals, orbitals), jnp.bfloat16),
            pltpu.VMEM((2 * orbitals, orbitals), jnp.float32),
        ],
    )


def fetch(part, parts, copies):
    @pl.when(part == 0)
    def _():
        for copy in sum(copies, []):
            copy.start()

    for p in range(parts):

        @pl.when(part == p)
        def _():
            for copy in copies[p]:
                copy.wait()


def add_corners(core, inner, outer, rim, total):
    orbitals, width = total.shape[-1], rim.shape[-1]
    for energy in range(2):
        for side in range(2):
            matrix = rim[0, side]
            corner = jnp.where(core == side, outer[energy, 0, 0], inner[energy, 0, 0])
            left = product(matrix, corner).astype(jnp.bfloat16)
            start = 0 if side == 0 else orbitals - width
            rows = slice(energy * orbitals + start, energy * orbitals + start + width)
            total[rows, start : start + width] += product_t(left, matrix)


def blended(ahead, lead, behind, trail):
    mixed = lead * ahead.astype(jnp.float32) + trail * behind.astype(jnp.float32)
    return mixed.astype(jnp.bfloat16)


def lesser_kernel(
    place, offsets, pattern, bose,
    own, first, second, inner, outer, couple, rim, out, kept, window, left, total, sems,
):
    cut, core = place[0], place[1]
    part = pl.program_id(0)
    orbitals = couple.shape[-1]
    fetch(
        part,
        2,
        [
            [
                pltpu.make_async_copy(own.at[:, 0, p], window.at[p, pl.ds(2, 2)], sems.at[p, 0]),
                pltpu.make_async_copy(
                    first.at[:, 0, p], window.at[p, pl.ds(4 * core, 2)], sems.at[p, 1]
                ),
                pltpu.make_async_copy(
                    second.at[:, 0, p], window.at[p, pl.ds(4 - 4 * core, 2)], sems.at[p, 2]
                ),
            ]
            for p in range(2)
        ],
    )
    here = window.at[part]
    total[...] = jnp.zeros_like(total)
    add_corners(core, inner, outer, rim, total)
    for mode in range(couple.shape[1]):

        @pl.when(pattern[cut, mode] > 0)
        def _():
            shift, matrix = offsets[mode], couple[0, mode]
            for energy in range(2):
                rows = slice(energy * orbitals, (energy + 1) * orbitals)
                mixed = blended(
                    here[2 + energy + shift], bose[mode] + 1.0, here[2 + energy - shift], bose[mode]
                )
                left[rows] = product(matrix, mixed).astype(jnp.bfloat16)
            total[...] += product_t(left[...], matrix)

    for energy in range(2):
        rows = slice(energy * orbitals, (energy + 1) * orbitals)
        out[energy, 0, 0] = total[rows].astype(jnp.bfloat16)
        kept[0, energy] = total[rows]


def greater_kernel(
    place, offsets, pattern, bose,
    own, first, second, inner, outer, low, couple, rim, kept, window, left, total, sems,
):
    cut, core = place[0], place[1]
    part = pl.program_id(0)
    orbitals = couple.shape[-1]
    fetch(
        part,
        2,
        [
            [
                pltpu.make_async_copy(own.at[:, 0, p], window.at[p, pl.ds(1, 2)], sems.at[p, 0]),
                pltpu.make_async_copy(first.at[0, 0, p], window.at[p, 3 * core], sems.at[p, 1]),
                pltpu.make_async_copy(second.at[0, 0, p], window.at[p, 3 - 3 * core], sems.at[p, 2]),
            ]
            for p in range(2)
        ],
    )
    here = window.at[part]
    total[...] = jnp.zeros_like(total)
    add_corners(core, inner, outer, rim, total)
    for mode in range(couple.shape[1]):
        active = pattern[cut, mode] > 0

        @pl.when(active & (offsets[mode] == 2))
        def _():
            matrix = couple[0, mode]
            for energy in range(2):
                rows = slice(energy * orbitals, (energy + 1) * orbitals)
                weight = bose[mode] + (0.0 if energy == 0 else 1.0)
                left[rows] = (product(matrix, here[3 - 3 * energy]) * weight).astype(jnp.bfloat16)
            total[...] += product_t(left[...], matrix)

        @pl.when(active & (offsets[mode] != 2))
        def _():
            matrix = couple[0, mode]
            for energy in range(2):
                rows = slice(energy * orbitals, (energy + 1) * orbitals)
                mixed = blended(here[2 + energy], bose[mode], here[energy], bose[mode] + 1.0)
                left[rows] = product(matrix, mixed).astype(jnp.bfloat16)
            total[...] += product_t(left[...], matrix)

    for energy in range(2):
        rows = slice(energy * orbitals, (energy + 1) * orbitals)
        kept[energy, 0, 0] = (0.5 * (total[rows] - low[0, energy])).astype(kept.dtype)


def product_specs(kind, slots, couplings, rim_couple):
    modes, orbitals = couplings.shape[1], couplings.shape[2]
    width = rim_couple.shape[-1]
    corner = pl.BlockSpec((2, 1, 1, width, width), lambda p, *_: (0, kind, p, 0, 0))
    matrices = [
        pl.BlockSpec((1, modes, orbitals, orbitals), lambda p, *_: (0, 0, 0, 0)),
        pl.BlockSpec((1, 2, width, width), lambda p, *_: (0, 0, 0, 0)),
    ]
    scratch = [
        pltpu.VMEM((2, slots, orbitals, orbitals), jnp.bfloat16),
        pltpu.VMEM((2 * orbitals, orbitals), jnp.bfloat16),
        pltpu.VMEM((2 * orbitals, orbitals), jnp.float32),
        pltpu.SemaphoreType.DMA((2, 3)),
    ]
    kept = pl.BlockSpec((1, 2, orbitals, orbitals), lambda p, *_: (p, 0, 0, 0))
    return [pl.BlockSpec(memory_space=pl.ANY)] * 3 + [corner, corner], matrices, kept, scratch


def lesser_terms(scalars, bose, lesser, first, second, corners, couplings, rim_couple):
    parts, orbitals = lesser.shape[2], lesser.shape[-1]
    inputs, matrices, kept, scratch = product_specs(0, 6, couplings, rim_couple)
    return call(
        lesser_kernel,
        "lesser_terms",
        (*scalars, bose),
        (lesser, first, second, *corners, couplings, rim_couple),
        (parts,),
        inputs + matrices,
        [pl.BlockSpec((2, 1, 1, orbitals, orbitals), lambda p, *_: (0, 0, p, 0, 0)), kept],
        [
            jax.ShapeDtypeStruct(lesser.shape, jnp.bfloat16),
            jax.ShapeDtypeStruct((parts, 2, orbitals, orbitals), jnp.float32),
        ],
        60,
        12 * 8 * orbitals**3,
        scratch=scratch,
    )


def greater_terms(scalars, bose, greater, first, second, corners, low, couplings, rim_couple):
    parts, orbitals = greater.shape[2], greater.shape[-1]
    inputs, matrices, kept, scratch = product_specs(1, 4, couplings, rim_couple)
    return call(
        greater_kernel,
        "greater_terms",
        (*scalars, bose),
        (greater, first, second, *corners, low, couplings, rim_couple),
        (parts,),
        inputs + [kept] + matrices,
        pl.BlockSpec((2, 1, 1, orbitals, orbitals), lambda p, *_: (0, 0, p, 0, 0)),
        jax.ShapeDtypeStruct(greater.shape, jnp.bfloat16),
        60,
        12 * 8 * orbitals**3,
        scratch=scratch,
    )


def added(near, at, far):
    slab = lax.dynamic_index_in_dim(near, at, 0, keepdims=True)
    slab = (slab.astype(jnp.float32) + far[None, None].astype(jnp.float32)).astype(near.dtype)
    return lax.dynamic_update_slice_in_dim(near, slab, at, 0)


def body(lesser, greater, couplings, rim_couple, bose_factor, offsets, pattern):
    energies = lax.axis_size("energy")
    cuts = lax.axis_size("cuts")
    width = rim_couple.shape[-1]
    core = lax.axis_index("cuts") & 1

    outer = swapped(cornered(False, width, lesser, greater), energies, cuts, False)
    place, lesser_sent = lax.optimization_barrier((placed(), lesser))
    low = [shifted(lesser_sent, energies, cuts, first) for first in (True, False)]
    near = [lax.dynamic_slice_in_dim(greater, at, 1, 0) for at in (1 - core, core)]
    outer, place = lax.optimization_barrier((outer, place))
    high = [shifted(term, energies, cuts, i == 0) for i, term in enumerate(near)]
    scalars = (place, offsets, pattern)

    first, second = far_terms(scalars, bose_factor, greater, couplings)
    second, lesser_corner = lax.optimization_barrier((second, lesser))
    inner = swapped(cornered(True, width, lesser_corner, greater), energies, cuts, True)
    inner, first = lax.optimization_barrier((inner, first))
    corners = (inner, outer)
    first = shifted(first, energies, cuts, True)
    low, second = lax.optimization_barrier((low, second))
    second = shifted(second, energies, cuts, False)

    low_out, low_kept = lesser_terms(
        scalars, bose_factor, lesser, *low, corners, couplings, rim_couple
    )
    kept = greater_terms(
        scalars, bose_factor, greater, *high, corners, low_kept, couplings, rim_couple
    )
    return low_out, added(added(kept, core, first), 1 - core, second)


def solution(mesh):
    return jax.shard_map(
        body,
        mesh=mesh,
        in_specs=(
            P("energy", "cuts", None, None, None),
            P("energy", "cuts", None, None, None),
            P("cuts", None, None, None),
            P("cuts", None, None, None),
            P(),
            P(),
            P(),
        ),
        out_specs=(P("energy", "cuts", None, None, None), P("energy", "cuts", None, None, None)),
        check_vma=False,
    )
```

```python
import jax
import jax.numpy as jnp
from jax import lax
from jax.experimental import pallas as pl
from jax.experimental.pallas import tpu as pltpu
from jax.sharding import PartitionSpec as P


def shifted(x, energies, cuts, first):
    pairs = []
    for e in range(energies):
        for c in range(cuts):
            up = (c % 2 == 0) == first
            to = e + 1 if up else e - 1
            if 0 <= to < energies:
                pairs.append((e * cuts + c, to * cuts + c))
    return lax.ppermute(x, ("energy", "cuts"), pairs)


def swapped(x, energies, cuts, inside):
    pairs = []
    for e in range(energies):
        for c in range(cuts):
            to = c ^ 1 if inside else (c + 1 if c % 2 else c - 1)
            if 0 <= to < cuts:
                pairs.append((e * cuts + c, e * cuts + to))
    return lax.ppermute(x, ("energy", "cuts"), pairs)


def product(a, b):
    return lax.dot_general(a, b, (((1,), (0,)), ((), ())), preferred_element_type=jnp.float32)


def product_t(a, b):
    return lax.dot_general(a, b, (((1,), (1,)), ((), ())), preferred_element_type=jnp.float32)


def call(kernel, name, scalars, operands, grid, in_specs, out_specs, out_shape, vmem, flops, **more):
    scratch = more.pop("scratch", [])
    return pl.pallas_call(
        kernel,
        grid_spec=pltpu.PrefetchScalarGridSpec(
            num_scalar_prefetch=len(scalars),
            grid=grid,
            in_specs=in_specs,
            out_specs=out_specs,
            scratch_shapes=scratch,
        ),
        out_shape=out_shape,
        compiler_params=pltpu.CompilerParams(vmem_limit_bytes=vmem * 2**20),
        cost_estimate=pl.CostEstimate(flops=flops, bytes_accessed=4 * 2**20, transcendentals=0),
        name=name,
        **more,
    )(*scalars, *operands)


def corner_kernel(inside, low_top, high_top, low_bottom, high_bottom, out):
    core = lax.axis_index("cuts") & 1
    for kind, (top, bottom) in enumerate(((low_top, low_bottom), (high_top, high_bottom))):
        upper = core == 1 if inside else core == 0
        out[:, kind] = jnp.where(upper, top[:, 0], bottom[:, 0])


def cornered(inside, width, lesser, greater):
    parts = lesser.shape[2]
    last = lesser.shape[-1] // width - 1
    shape = (2, 2, parts, width, width)
    block = (2, 1, parts, width, width)
    top = pl.BlockSpec(block, lambda i: (0, 0, 0, 0, 0))
    bottom = pl.BlockSpec(block, lambda i: (0, 0, 0, last, last))
    return call(
        lambda *refs: corner_kernel(inside, *refs),
        "cornered",
        (),
        (lesser, greater, lesser, greater),
        (1,),
        [top, top, bottom, bottom],
        pl.BlockSpec(shape, lambda i: (0, 0, 0, 0, 0)),
        jax.ShapeDtypeStruct(shape, lesser.dtype),
        60,
        0,
    )


def place_kernel(out):
    cut = lax.axis_index("cuts")
    out[0] = cut
    out[1] = cut & 1


def placed():
    return call(
        place_kernel,
        "placed",
        (),
        (),
        (),
        [],
        pl.BlockSpec(memory_space=pltpu.SMEM),
        jax.ShapeDtypeStruct((2,), jnp.int32),
        60,
        10**12,
    )


def far_kernel(place, offsets, pattern, bose, green, couple, first_out, second_out, left, total):
    cut, core = place[0], place[1]
    orbitals = couple.shape[-1]
    total[...] = jnp.zeros_like(total)
    for mode in range(couple.shape[1]):

        @pl.when((pattern[cut, mode] > 0) & (offsets[mode] == 2))
        def _():
            matrix = couple[0, mode]
            for energy in range(2):
                weight = bose[mode] + (1.0 if energy == 0 else 0.0)
                rows = slice(energy * orbitals, (energy + 1) * orbitals)
                left[rows] = (product(matrix, green[energy, 0, 0]) * weight).astype(jnp.bfloat16)
            total[...] += product_t(left[...], matrix)

    for slot, out in enumerate((first_out, second_out)):
        start = pl.multiple_of((core if slot == 0 else 1 - core) * orbitals, orbitals)
        out[0] = (0.5 * total[pl.ds(start, orbitals)]).astype(jnp.bfloat16)


def far_terms(scalars, bose, greater, couplings):
    parts, orbitals = greater.shape[2], greater.shape[-1]
    modes = couplings.shape[1]
    whole = pl.BlockSpec((1, orbitals, orbitals), lambda p, *_: (p, 0, 0))
    return call(
        far_kernel,
        "far_terms",
        (*scalars, bose),
        (greater, couplings),
        (parts,),
        [
            pl.BlockSpec((2, 1, 1, orbitals, orbitals), lambda p, *_: (0, 0, p, 0, 0)),
            pl.BlockSpec((1, modes, orbitals, orbitals), lambda p, *_: (0, 0, 0, 0)),
        ],
        [whole, whole],
        [jax.ShapeDtypeStruct((parts, orbitals, orbitals), jnp.bfloat16)] * 2,
        60,
        64 * modes * orbitals**3,
        scratch=[
            pltpu.VMEM((2 * orbitals, orbitals), jnp.bfloat16),
            pltpu.VMEM((2 * orbitals, orbitals), jnp.float32),
        ],
    )


def fetch(part, parts, copies):
    @pl.when(part == 0)
    def _():
        for copy in sum(copies, []):
            copy.start()

    for p in range(parts):

        @pl.when(part == p)
        def _():
            for copy in copies[p]:
                copy.wait()


def add_corners(core, inner, outer, rim, total):
    orbitals, width = total.shape[-1], rim.shape[-1]
    for energy in range(2):
        for side in range(2):
            matrix = rim[0, side]
            corner = jnp.where(core == side, outer[energy, 0, 0], inner[energy, 0, 0])
            left = product(matrix, corner).astype(jnp.bfloat16)
            start = 0 if side == 0 else orbitals - width
            rows = slice(energy * orbitals + start, energy * orbitals + start + width)
            total[rows, start : start + width] += product_t(left, matrix)


def blended(ahead, lead, behind, trail):
    mixed = lead * ahead.astype(jnp.float32) + trail * behind.astype(jnp.float32)
    return mixed.astype(jnp.bfloat16)


def lesser_kernel(
    place, offsets, pattern, bose,
    own, first, second, inner, outer, couple, rim, out, kept, window, left, total, sems,
):
    cut, core = place[0], place[1]
    part = pl.program_id(0)
    orbitals = couple.shape[-1]
    fetch(
        part,
        2,
        [
            [
                pltpu.make_async_copy(own.at[:, 0, p], window.at[p, pl.ds(2, 2)], sems.at[p, 0]),
                pltpu.make_async_copy(
                    first.at[:, 0, p], window.at[p, pl.ds(4 * core, 2)], sems.at[p, 1]
                ),
                pltpu.make_async_copy(
                    second.at[:, 0, p], window.at[p, pl.ds(4 - 4 * core, 2)], sems.at[p, 2]
                ),
            ]
            for p in range(2)
        ],
    )
    here = window.at[part]
    total[...] = jnp.zeros_like(total)
    add_corners(core, inner, outer, rim, total)
    for mode in range(couple.shape[1]):

        @pl.when(pattern[cut, mode] > 0)
        def _():
            shift, matrix = offsets[mode], couple[0, mode]
            for energy in range(2):
                rows = slice(energy * orbitals, (energy + 1) * orbitals)
                mixed = blended(
                    here[2 + energy + shift], bose[mode] + 1.0, here[2 + energy - shift], bose[mode]
                )
                left[rows] = product(matrix, mixed).astype(jnp.bfloat16)
            total[...] += product_t(left[...], matrix)

    for energy in range(2):
        rows = slice(energy * orbitals, (energy + 1) * orbitals)
        out[energy, 0, 0] = total[rows].astype(jnp.bfloat16)
        kept[0, energy] = total[rows]


def greater_kernel(
    place, offsets, pattern, bose,
    own, first, second, inner, outer, low, couple, rim, kept, window, left, total, sems,
):
    cut, core = place[0], place[1]
    part = pl.program_id(0)
    orbitals = couple.shape[-1]
    fetch(
        part,
        2,
        [
            [
                pltpu.make_async_copy(own.at[:, 0, p], window.at[p, pl.ds(1, 2)], sems.at[p, 0]),
                pltpu.make_async_copy(first.at[0, 0, p], window.at[p, 3 * core], sems.at[p, 1]),
                pltpu.make_async_copy(second.at[0, 0, p], window.at[p, 3 - 3 * core], sems.at[p, 2]),
            ]
            for p in range(2)
        ],
    )
    here = window.at[part]
    total[...] = jnp.zeros_like(total)
    add_corners(core, inner, outer, rim, total)
    for mode in range(couple.shape[1]):
        active = pattern[cut, mode] > 0

        @pl.when(active & (offsets[mode] == 2))
        def _():
            matrix = couple[0, mode]
            for energy in range(2):
                rows = slice(energy * orbitals, (energy + 1) * orbitals)
                weight = bose[mode] + (0.0 if energy == 0 else 1.0)
                left[rows] = (product(matrix, here[3 - 3 * energy]) * weight).astype(jnp.bfloat16)
            total[...] += product_t(left[...], matrix)

        @pl.when(active & (offsets[mode] != 2))
        def _():
            matrix = couple[0, mode]
            for energy in range(2):
                rows = slice(energy * orbitals, (energy + 1) * orbitals)
                mixed = blended(here[2 + energy], bose[mode], here[energy], bose[mode] + 1.0)
                left[rows] = product(matrix, mixed).astype(jnp.bfloat16)
            total[...] += product_t(left[...], matrix)

    for energy in range(2):
        rows = slice(energy * orbitals, (energy + 1) * orbitals)
        kept[energy, 0, 0] = (0.5 * (total[rows] - low[0, energy])).astype(kept.dtype)


def product_specs(kind, slots, couplings, rim_couple):
    modes, orbitals = couplings.shape[1], couplings.shape[2]
    width = rim_couple.shape[-1]
    corner = pl.BlockSpec((2, 1, 1, width, width), lambda p, *_: (0, kind, p, 0, 0))
    matrices = [
        pl.BlockSpec((1, modes, orbitals, orbitals), lambda p, *_: (0, 0, 0, 0)),
        pl.BlockSpec((1, 2, width, width), lambda p, *_: (0, 0, 0, 0)),
    ]
    scratch = [
        pltpu.VMEM((2, slots, orbitals, orbitals), jnp.bfloat16),
        pltpu.VMEM((2 * orbitals, orbitals), jnp.bfloat16),
        pltpu.VMEM((2 * orbitals, orbitals), jnp.float32),
        pltpu.SemaphoreType.DMA((2, 3)),
    ]
    kept = pl.BlockSpec((1, 2, orbitals, orbitals), lambda p, *_: (p, 0, 0, 0))
    return [pl.BlockSpec(memory_space=pl.ANY)] * 3 + [corner, corner], matrices, kept, scratch


def lesser_terms(scalars, bose, lesser, first, second, corners, couplings, rim_couple):
    parts, orbitals = lesser.shape[2], lesser.shape[-1]
    inputs, matrices, kept, scratch = product_specs(0, 6, couplings, rim_couple)
    return call(
        lesser_kernel,
        "lesser_terms",
        (*scalars, bose),
        (lesser, first, second, *corners, couplings, rim_couple),
        (parts,),
        inputs + matrices,
        [pl.BlockSpec((2, 1, 1, orbitals, orbitals), lambda p, *_: (0, 0, p, 0, 0)), kept],
        [
            jax.ShapeDtypeStruct(lesser.shape, jnp.bfloat16),
            jax.ShapeDtypeStruct((parts, 2, orbitals, orbitals), jnp.float32),
        ],
        60,
        12 * 8 * orbitals**3,
        scratch=scratch,
    )


def greater_terms(scalars, bose, greater, first, second, corners, low, couplings, rim_couple):
    parts, orbitals = greater.shape[2], greater.shape[-1]
    inputs, matrices, kept, scratch = product_specs(1, 4, couplings, rim_couple)
    return call(
        greater_kernel,
        "greater_terms",
        (*scalars, bose),
        (greater, first, second, *corners, low, couplings, rim_couple),
        (parts,),
        inputs + [kept] + matrices,
        pl.BlockSpec((2, 1, 1, orbitals, orbitals), lambda p, *_: (0, 0, p, 0, 0)),
        jax.ShapeDtypeStruct(greater.shape, jnp.bfloat16),
        60,
        12 * 8 * orbitals**3,
        scratch=scratch,
    )


def added(near, at, far):
    slab = lax.dynamic_index_in_dim(near, at, 0, keepdims=True)
    slab = (slab.astype(jnp.float32) + far[None, None].astype(jnp.float32)).astype(near.dtype)
    return lax.dynamic_update_slice_in_dim(near, slab, at, 0)


def last_kernel(place, near, far, partial, out, mixed, sems):
    energy = 1 - place[1]
    parts, orbitals = mixed.shape[0], mixed.shape[1]
    rows = orbitals // 2
    copies = []
    for part in range(parts):
        for half in range(2):
            at = slice(half * rows, (half + 1) * rows)
            value = near[part, at].astype(jnp.float32) + far[part, at].astype(jnp.float32)
            mixed[part, at] = value.astype(mixed.dtype)
            copy = pltpu.make_async_copy(
                mixed.at[part, pl.ds(half * rows, rows)],
                out.at[energy, 0, part, pl.ds(half * rows, rows)],
                sems.at[part, half],
            )
            copy.start()
            copies.append(copy)
    for copy in copies:
        copy.wait()


def last_added(place, near, far, partial):
    inside = pl.BlockSpec(memory_space=pltpu.VMEM)
    anywhere = pl.BlockSpec(memory_space=pl.ANY)
    return call(
        last_kernel,
        "last_added",
        (place,),
        (near, far, partial),
        (),
        [inside, inside, anywhere],
        anywhere,
        jax.ShapeDtypeStruct(partial.shape, partial.dtype),
        48,
        10**9,
        scratch=[
            pltpu.VMEM(near.shape, near.dtype),
            pltpu.SemaphoreType.DMA((near.shape[0], 2)),
        ],
        input_output_aliases={3: 0},
    )


def body(lesser, greater, couplings, rim_couple, bose_factor, offsets, pattern):
    energies = lax.axis_size("energy")
    cuts = lax.axis_size("cuts")
    width = rim_couple.shape[-1]
    core = lax.axis_index("cuts") & 1

    outer = swapped(cornered(False, width, lesser, greater), energies, cuts, False)
    place, lesser_sent = lax.optimization_barrier((placed(), lesser))
    low = [shifted(lesser_sent, energies, cuts, first) for first in (True, False)]
    near = [lax.dynamic_slice_in_dim(greater, at, 1, 0) for at in (1 - core, core)]
    outer, place = lax.optimization_barrier((outer, place))
    high = [shifted(term, energies, cuts, i == 0) for i, term in enumerate(near)]
    scalars = (place, offsets, pattern)

    first, second = far_terms(scalars, bose_factor, greater, couplings)
    second, lesser_corner = lax.optimization_barrier((second, lesser))
    inner = swapped(cornered(True, width, lesser_corner, greater), energies, cuts, True)
    inner, first = lax.optimization_barrier((inner, first))
    corners = (inner, outer)
    first = shifted(first, energies, cuts, True)
    low, second = lax.optimization_barrier((low, second))
    second = shifted(second, energies, cuts, False)

    low_out, low_kept = lesser_terms(
        scalars, bose_factor, lesser, *low, corners, couplings, rim_couple
    )
    kept = greater_terms(
        scalars, bose_factor, greater, *high, corners, low_kept, couplings, rim_couple
    )
    later = lax.dynamic_index_in_dim(kept, 1 - core, 0, keepdims=False)[0]
    return low_out, last_added(place, later, second, added(kept, core, first))


def solution(mesh):
    return jax.shard_map(
        body,
        mesh=mesh,
        in_specs=(
            P("energy", "cuts", None, None, None),
            P("energy", "cuts", None, None, None),
            P("cuts", None, None, None),
            P("cuts", None, None, None),
            P(),
            P(),
            P(),
        ),
        out_specs=(P("energy", "cuts", None, None, None), P("energy", "cuts", None, None, None)),
        check_vma=False,
    )
```

```python
import jax
import jax.numpy as jnp
from jax import lax
from jax.experimental import pallas as pl
from jax.experimental.pallas import tpu as pltpu
from jax.sharding import PartitionSpec as P


def shifted(x, energies, cuts, first):
    pairs = []
    for e in range(energies):
        for c in range(cuts):
            up = (c % 2 == 0) == first
            to = e + 1 if up else e - 1
            if 0 <= to < energies:
                pairs.append((e * cuts + c, to * cuts + c))
    return lax.ppermute(x, ("energy", "cuts"), pairs)


def swapped(x, energies, cuts, inside):
    pairs = []
    for e in range(energies):
        for c in range(cuts):
            to = c ^ 1 if inside else (c + 1 if c % 2 else c - 1)
            if 0 <= to < cuts:
                pairs.append((e * cuts + c, e * cuts + to))
    return lax.ppermute(x, ("energy", "cuts"), pairs)


def product(a, b):
    return lax.dot_general(a, b, (((1,), (0,)), ((), ())), preferred_element_type=jnp.float32)


def product_t(a, b):
    return lax.dot_general(a, b, (((1,), (1,)), ((), ())), preferred_element_type=jnp.float32)


def call(kernel, name, scalars, operands, grid, in_specs, out_specs, out_shape, vmem, flops, **more):
    scratch = more.pop("scratch", [])
    return pl.pallas_call(
        kernel,
        grid_spec=pltpu.PrefetchScalarGridSpec(
            num_scalar_prefetch=len(scalars),
            grid=grid,
            in_specs=in_specs,
            out_specs=out_specs,
            scratch_shapes=scratch,
        ),
        out_shape=out_shape,
        compiler_params=pltpu.CompilerParams(vmem_limit_bytes=vmem * 2**20),
        cost_estimate=pl.CostEstimate(flops=flops, bytes_accessed=4 * 2**20, transcendentals=0),
        name=name,
        **more,
    )(*scalars, *operands)


def corner_kernel(inside, width, lesser, greater, out, sems):
    core = lax.axis_index("cuts") & 1
    last = (lesser.shape[-1] - width) // width
    upper = (1 - core if inside else core) * last
    edge = pl.ds(pl.multiple_of(upper * width, width), width)
    copies = [
        pltpu.make_async_copy(green.at[:, 0, :, edge, edge], out.at[:, kind], sems.at[kind])
        for kind, green in enumerate((lesser, greater))
    ]
    for copy in copies:
        copy.start()
    for copy in copies:
        copy.wait()


def cornered(inside, width, lesser, greater):
    shape = (2, 2, lesser.shape[2], width, width)
    anywhere = pl.BlockSpec(memory_space=pl.ANY)
    return call(
        lambda *refs: corner_kernel(inside, width, *refs),
        "cornered",
        (),
        (lesser, greater),
        (),
        [anywhere, anywhere],
        pl.BlockSpec(memory_space=pltpu.VMEM),
        jax.ShapeDtypeStruct(shape, lesser.dtype),
        58,
        0,
        scratch=[pltpu.SemaphoreType.DMA((2,))],
    )


def place_kernel(out):
    cut = lax.axis_index("cuts")
    out[0] = cut
    out[1] = cut & 1


def placed():
    return call(
        place_kernel,
        "placed",
        (),
        (),
        (),
        [],
        pl.BlockSpec(memory_space=pltpu.SMEM),
        jax.ShapeDtypeStruct((2,), jnp.int32),
        60,
        10**12,
    )


def far_kernel(place, offsets, pattern, bose, green, couple, first_out, second_out, left, total):
    cut, core = place[0], place[1]
    orbitals = couple.shape[-1]
    total[...] = jnp.zeros_like(total)
    for mode in range(couple.shape[1]):

        @pl.when((pattern[cut, mode] > 0) & (offsets[mode] == 2))
        def _():
            matrix = couple[0, mode]
            for energy in range(2):
                weight = bose[mode] + (1.0 if energy == 0 else 0.0)
                rows = slice(energy * orbitals, (energy + 1) * orbitals)
                left[rows] = (product(matrix, green[energy, 0, 0]) * weight).astype(jnp.bfloat16)
            total[...] += product_t(left[...], matrix)

    for slot, out in enumerate((first_out, second_out)):
        start = pl.multiple_of((core if slot == 0 else 1 - core) * orbitals, orbitals)
        out[0] = (0.5 * total[pl.ds(start, orbitals)]).astype(jnp.bfloat16)


def far_terms(scalars, bose, greater, couplings):
    parts, orbitals = greater.shape[2], greater.shape[-1]
    modes = couplings.shape[1]
    whole = pl.BlockSpec((1, orbitals, orbitals), lambda p, *_: (p, 0, 0))
    return call(
        far_kernel,
        "far_terms",
        (*scalars, bose),
        (greater, couplings),
        (parts,),
        [
            pl.BlockSpec((2, 1, 1, orbitals, orbitals), lambda p, *_: (0, 0, p, 0, 0)),
            pl.BlockSpec((1, modes, orbitals, orbitals), lambda p, *_: (0, 0, 0, 0)),
        ],
        [whole, whole],
        [jax.ShapeDtypeStruct((parts, orbitals, orbitals), jnp.bfloat16)] * 2,
        60,
        64 * modes * orbitals**3,
        scratch=[
            pltpu.VMEM((2 * orbitals, orbitals), jnp.bfloat16),
            pltpu.VMEM((2 * orbitals, orbitals), jnp.float32),
        ],
    )


def fetch(part, parts, copies):
    @pl.when(part == 0)
    def _():
        for copy in sum(copies, []):
            copy.start()

    for p in range(parts):

        @pl.when(part == p)
        def _():
            for copy in copies[p]:
                copy.wait()


def add_corners(core, inner, outer, rim, total):
    orbitals, width = total.shape[-1], rim.shape[-1]
    for energy in range(2):
        for side in range(2):
            matrix = rim[0, side]
            corner = jnp.where(core == side, outer[energy, 0, 0], inner[energy, 0, 0])
            left = product(matrix, corner).astype(jnp.bfloat16)
            start = 0 if side == 0 else orbitals - width
            rows = slice(energy * orbitals + start, energy * orbitals + start + width)
            total[rows, start : start + width] += product_t(left, matrix)


def blended(ahead, lead, behind, trail):
    mixed = lead * ahead.astype(jnp.float32) + trail * behind.astype(jnp.float32)
    return mixed.astype(jnp.bfloat16)


def lesser_kernel(
    place, offsets, pattern, bose,
    own, first, second, inner, outer, couple, rim, out, kept, window, left, total, sems,
):
    cut, core = place[0], place[1]
    part = pl.program_id(0)
    orbitals = couple.shape[-1]
    fetch(
        part,
        2,
        [
            [
                pltpu.make_async_copy(own.at[:, 0, p], window.at[p, pl.ds(2, 2)], sems.at[p, 0]),
                pltpu.make_async_copy(
                    first.at[:, 0, p], window.at[p, pl.ds(4 * core, 2)], sems.at[p, 1]
                ),
                pltpu.make_async_copy(
                    second.at[:, 0, p], window.at[p, pl.ds(4 - 4 * core, 2)], sems.at[p, 2]
                ),
            ]
            for p in range(2)
        ],
    )
    here = window.at[part]
    total[...] = jnp.zeros_like(total)
    add_corners(core, inner, outer, rim, total)
    for mode in range(couple.shape[1]):

        @pl.when(pattern[cut, mode] > 0)
        def _():
            shift, matrix = offsets[mode], couple[0, mode]
            for energy in range(2):
                rows = slice(energy * orbitals, (energy + 1) * orbitals)
                mixed = blended(
                    here[2 + energy + shift], bose[mode] + 1.0, here[2 + energy - shift], bose[mode]
                )
                left[rows] = product(matrix, mixed).astype(jnp.bfloat16)
            total[...] += product_t(left[...], matrix)

    for energy in range(2):
        rows = slice(energy * orbitals, (energy + 1) * orbitals)
        out[energy, 0, 0] = total[rows].astype(jnp.bfloat16)
        kept[0, energy] = total[rows]


def greater_kernel(
    place, offsets, pattern, bose,
    own, first, second, inner, outer, low, couple, rim, kept, window, left, total, sems,
):
    cut, core = place[0], place[1]
    part = pl.program_id(0)
    orbitals = couple.shape[-1]
    fetch(
        part,
        2,
        [
            [
                pltpu.make_async_copy(own.at[:, 0, p], window.at[p, pl.ds(1, 2)], sems.at[p, 0]),
                pltpu.make_async_copy(first.at[0, 0, p], window.at[p, 3 * core], sems.at[p, 1]),
                pltpu.make_async_copy(second.at[0, 0, p], window.at[p, 3 - 3 * core], sems.at[p, 2]),
            ]
            for p in range(2)
        ],
    )
    here = window.at[part]
    total[...] = jnp.zeros_like(total)
    add_corners(core, inner, outer, rim, total)
    for mode in range(couple.shape[1]):
        active = pattern[cut, mode] > 0

        @pl.when(active & (offsets[mode] == 2))
        def _():
            matrix = couple[0, mode]
            for energy in range(2):
                rows = slice(energy * orbitals, (energy + 1) * orbitals)
                weight = bose[mode] + (0.0 if energy == 0 else 1.0)
                left[rows] = (product(matrix, here[3 - 3 * energy]) * weight).astype(jnp.bfloat16)
            total[...] += product_t(left[...], matrix)

        @pl.when(active & (offsets[mode] != 2))
        def _():
            matrix = couple[0, mode]
            for energy in range(2):
                rows = slice(energy * orbitals, (energy + 1) * orbitals)
                mixed = blended(here[2 + energy], bose[mode], here[energy], bose[mode] + 1.0)
                left[rows] = product(matrix, mixed).astype(jnp.bfloat16)
            total[...] += product_t(left[...], matrix)

    for energy in range(2):
        rows = slice(energy * orbitals, (energy + 1) * orbitals)
        kept[energy, 0, 0] = (0.5 * (total[rows] - low[0, energy])).astype(kept.dtype)


def product_specs(kind, slots, couplings, rim_couple):
    modes, orbitals = couplings.shape[1], couplings.shape[2]
    width = rim_couple.shape[-1]
    corner = pl.BlockSpec((2, 1, 1, width, width), lambda p, *_: (0, kind, p, 0, 0))
    matrices = [
        pl.BlockSpec((1, modes, orbitals, orbitals), lambda p, *_: (0, 0, 0, 0)),
        pl.BlockSpec((1, 2, width, width), lambda p, *_: (0, 0, 0, 0)),
    ]
    scratch = [
        pltpu.VMEM((2, slots, orbitals, orbitals), jnp.bfloat16),
        pltpu.VMEM((2 * orbitals, orbitals), jnp.bfloat16),
        pltpu.VMEM((2 * orbitals, orbitals), jnp.float32),
        pltpu.SemaphoreType.DMA((2, 3)),
    ]
    kept = pl.BlockSpec((1, 2, orbitals, orbitals), lambda p, *_: (p, 0, 0, 0))
    return [pl.BlockSpec(memory_space=pl.ANY)] * 3 + [corner, corner], matrices, kept, scratch


def lesser_terms(scalars, bose, lesser, first, second, corners, couplings, rim_couple):
    parts, orbitals = lesser.shape[2], lesser.shape[-1]
    inputs, matrices, kept, scratch = product_specs(0, 6, couplings, rim_couple)
    return call(
        lesser_kernel,
        "lesser_terms",
        (*scalars, bose),
        (lesser, first, second, *corners, couplings, rim_couple),
        (parts,),
        inputs + matrices,
        [pl.BlockSpec((2, 1, 1, orbitals, orbitals), lambda p, *_: (0, 0, p, 0, 0)), kept],
        [
            jax.ShapeDtypeStruct(lesser.shape, jnp.bfloat16),
            jax.ShapeDtypeStruct((parts, 2, orbitals, orbitals), jnp.float32),
        ],
        60,
        12 * 8 * orbitals**3,
        scratch=scratch,
    )


def greater_terms(scalars, bose, greater, first, second, corners, low, couplings, rim_couple):
    parts, orbitals = greater.shape[2], greater.shape[-1]
    inputs, matrices, kept, scratch = product_specs(1, 4, couplings, rim_couple)
    return call(
        greater_kernel,
        "greater_terms",
        (*scalars, bose),
        (greater, first, second, *corners, low, couplings, rim_couple),
        (parts,),
        inputs + [kept] + matrices,
        pl.BlockSpec((2, 1, 1, orbitals, orbitals), lambda p, *_: (0, 0, p, 0, 0)),
        jax.ShapeDtypeStruct(greater.shape, jnp.bfloat16),
        60,
        12 * 8 * orbitals**3,
        scratch=scratch,
    )


def added(near, at, far):
    slab = lax.dynamic_index_in_dim(near, at, 0, keepdims=True)
    slab = (slab.astype(jnp.float32) + far[None, None].astype(jnp.float32)).astype(near.dtype)
    return lax.dynamic_update_slice_in_dim(near, slab, at, 0)


def last_kernel(place, near, far, partial, out, mixed, sems):
    energy = 1 - place[1]
    parts, orbitals = mixed.shape[0], mixed.shape[1]
    rows = orbitals // 4
    copies = []
    for part in range(parts):
        for half in range(4):
            at = slice(half * rows, (half + 1) * rows)
            value = near[part, at].astype(jnp.float32) + far[part, at].astype(jnp.float32)
            mixed[part, at] = value.astype(mixed.dtype)
            copy = pltpu.make_async_copy(
                mixed.at[part, pl.ds(half * rows, rows)],
                out.at[energy, 0, part, pl.ds(half * rows, rows)],
                sems.at[part, half],
            )
            copy.start()
            copies.append(copy)
    for copy in copies:
        copy.wait()


def last_added(place, near, far, partial):
    inside = pl.BlockSpec(memory_space=pltpu.VMEM)
    anywhere = pl.BlockSpec(memory_space=pl.ANY)
    return call(
        last_kernel,
        "last_added",
        (place,),
        (near, far, partial),
        (),
        [inside, inside, anywhere],
        anywhere,
        jax.ShapeDtypeStruct(partial.shape, partial.dtype),
        48,
        10**9,
        scratch=[
            pltpu.VMEM(near.shape, near.dtype),
            pltpu.SemaphoreType.DMA((near.shape[0], 4)),
        ],
        input_output_aliases={3: 0},
    )


def body(lesser, greater, couplings, rim_couple, bose_factor, offsets, pattern):
    energies = lax.axis_size("energy")
    cuts = lax.axis_size("cuts")
    width = rim_couple.shape[-1]
    core = lax.axis_index("cuts") & 1

    outer = swapped(cornered(False, width, lesser, greater), energies, cuts, False)
    place, lesser_sent = lax.optimization_barrier((placed(), lesser))
    low = [shifted(lesser_sent, energies, cuts, first) for first in (True, False)]
    near = [lax.dynamic_slice_in_dim(greater, at, 1, 0) for at in (1 - core, core)]
    outer, place = lax.optimization_barrier((outer, place))
    high = [shifted(term, energies, cuts, i == 0) for i, term in enumerate(near)]
    scalars = (place, offsets, pattern)

    first, second = far_terms(scalars, bose_factor, greater, couplings)
    second, lesser_corner = lax.optimization_barrier((second, lesser))
    inner = swapped(cornered(True, width, lesser_corner, greater), energies, cuts, True)
    inner, first = lax.optimization_barrier((inner, first))
    corners = (inner, outer)
    first = shifted(first, energies, cuts, True)
    low, second = lax.optimization_barrier((low, second))
    second = shifted(second, energies, cuts, False)

    low_out, low_kept = lesser_terms(
        scalars, bose_factor, lesser, *low, corners, couplings, rim_couple
    )
    kept = greater_terms(
        scalars, bose_factor, greater, *high, corners, low_kept, couplings, rim_couple
    )
    later = lax.dynamic_index_in_dim(kept, 1 - core, 0, keepdims=False)[0]
    return low_out, last_added(place, later, second, added(kept, core, first))


def solution(mesh):
    return jax.shard_map(
        body,
        mesh=mesh,
        in_specs=(
            P("energy", "cuts", None, None, None),
            P("energy", "cuts", None, None, None),
            P("cuts", None, None, None),
            P("cuts", None, None, None),
            P(),
            P(),
            P(),
        ),
        out_specs=(P("energy", "cuts", None, None, None), P("energy", "cuts", None, None, None)),
        check_vma=False,
    )
```
